32 devices in a mesh: dp: 4 (over y, x), tensor: 8 (over z, core).
Axes of the slice: x: 2, y: 2, z: 4, core: 2. Of those that a mesh axis runs over, the one named last changes fastest.
Arguments:
- tokens: bfloat16 [1024, 4096], P(('dp', 'tensor')), may hold values from -6 to 6
- cotangent: bfloat16 [1024, 4096], P(('dp', 'tensor')), may hold values from -6 to 6
- gate_up: bfloat16 [2, 4096, 14336], P(None, 'dp', 'tensor'), may hold values from -0.09375 to 0.09375
- down_weight: bfloat16 [14336, 4096], P('tensor'), may hold values from -0.046875 to 0.046875
- first_code: bfloat16 [2, 4096, 14336], P(None, 'dp', 'tensor'), may hold values from -1 to 1
- first_scale: float32 [2, 256, 112], P(None, 'dp', 'tensor'), may hold values from 0.05 to 0.5
- second_code: bfloat16 [2, 4096, 14336], P(None, 'dp', 'tensor'), may hold values from 0.049804688 to 1
- second_scale: float32 [2, 256, 112], P(None, 'dp', 'tensor'), may hold values from 0.005 to 0.05
Outputs:
- input_grad: bfloat16 [1024, 4096], P(('dp', 'tensor'))
- new_gate_up: bfloat16 [2, 4096, 14336], P(None, 'dp', 'tensor')
- new_first_code: bfloat16 [2, 4096, 14336], P(None, 'dp', 'tensor')
- new_first_scale: float32 [2, 256, 112], P(None, 'dp', 'tensor')
- new_second_code: bfloat16 [2, 4096, 14336], P(None, 'dp', 'tensor')
- new_second_scale: float32 [2, 256, 112], P(None, 'dp', 'tensor')
The draws below stay inside these ranges and needn't reach their ends.
All inputs are finite; a program needn't handle non-finite values. Where the reference program divides by a largest or mean magnitude, that divisor is 1e-20 or more.
Results may differ from the reference program's by a relative error of at most 0.023.
Values may be sent and summed in bfloat16 or wider, within the bound.
No kernel may reach another device: no remote copies, remote signals or barrier semaphores. Data moves between devices by JAX's collectives and lax.ppermute only.
A program may use at most 256 MiB of HBM per device.

```python
import math
import jax
import jax.numpy as jnp
from jax import lax

D = 4096
FF = 14336
TOKENS = 1024
N_DP = 4
N_TENSOR = 8


def block_scale(own_key, shape, cuts, smallest, high):
    def one(axis_at, parts):
        steps = jax.random.uniform(jax.random.fold_in(jax.random.fold_in(own_key, 6), axis_at), (parts,), jnp.float32, smallest / len(cuts), high / len(cuts))
        return jnp.repeat(jnp.exp(steps), shape[axis_at] // parts).reshape((-1,) + (1,) * (len(shape) - axis_at - 1))

    gain = one(*cuts[0])
    for cut in cuts[1:]:
        gain = gain * one(*cut)
    return gain


def centred(rng, shape, deviation, bound, cuts=(), dtype=jnp.bfloat16):
    factor_of = block_scale(rng, shape, cuts, -0.22, 0.18) if cuts else 1.0
    drawn = jax.random.normal(rng, shape, jnp.float32) * deviation * factor_of
    return jnp.minimum(jnp.maximum(drawn, -bound), bound).astype(dtype)


def setup_inputs(seed: int = 0) -> dict:
    splits = jax.random.split(jax.random.key(seed), 9)
    tokens = centred(splits[0], (TOKENS, D), 1.0, 6.0, ((0, 32),))
    cotangent = centred(splits[1], (TOKENS, D), 1.0, 6.0, ((0, 32),))
    gate_up = centred(splits[2], (2, D, FF), D ** -0.5, 0.09375, ((1, 4), (2, 8)))
    down_weight = centred(splits[3], (FF, D), FF ** -0.5, 0.046875, ((0, 8),))
    first_code = jnp.clip(jax.random.uniform(splits[4], (2, D, FF), jnp.float32, -1.0, 1.0) * block_scale(splits[4], (2, D, FF), ((1, 4), (2, 8)), -0.4, 0.0), -1.0, 1.0).astype(jnp.bfloat16)
    first_scale = jnp.clip(jnp.exp(math.log(0.5) - 2.3025851 * jax.random.uniform(splits[5], (2, D // 16, FF // 128), jnp.float32) ** block_scale(splits[5], (2, D // 16, FF // 128), ((1, 4), (2, 8)), -0.2, 0.2)), 0.05, 0.5)
    second_code = jnp.clip(0.049804688 + 0.9501953 * jax.random.uniform(splits[6], (2, D, FF), jnp.float32) ** block_scale(splits[6], (2, D, FF), ((1, 4), (2, 8)), -0.2, 0.2), 0.049804688, 1.0).astype(jnp.bfloat16)
    second_scale = jnp.clip(jnp.exp(math.log(0.05) - 2.3025851 * jax.random.uniform(splits[7], (2, D // 16, FF // 128), jnp.float32) ** block_scale(splits[7], (2, D // 16, FF // 128), ((1, 4), (2, 8)), -0.2, 0.2)), 0.005, 0.05)
    return {"tokens": tokens, "cotangent": cotangent, "gate_up": gate_up, "down_weight": down_weight, "first_code": first_code, "first_scale": first_scale, "second_code": second_code, "second_scale": second_scale}


learning_rate = 0.003
beta_first = 0.9
beta_second = 0.95

def dequantize(code, scale):
    shape = code.shape
    blocks = code.astype(jnp.float32).reshape(shape[0], shape[1] // 16, 16, shape[2] // 128, 128)
    return (blocks * scale[:, :, None, :, None]).reshape(shape)

def requantize(state):
    shape = state.shape
    blocks = state.reshape(shape[0], shape[1] // 16, 16, shape[2] // 128, 128)
    peak = lax.optimization_barrier(jnp.max(jnp.abs(blocks), axis=(2, 4))) + 1e-06
    code = (blocks / peak[:, :, None, :, None]).reshape(shape).astype(jnp.bfloat16)
    return (code, peak)

def optimizer(weights, first_code, first_scale, second_code, second_scale, grad):
    first = beta_first * dequantize(first_code, first_scale) + (1.0 - beta_first) * grad
    second = beta_second * dequantize(second_code, second_scale) + (1.0 - beta_second) * grad * grad
    updated = (weights.astype(jnp.float32) - learning_rate * first / (jnp.sqrt(second) + 1e-08)).astype(jnp.bfloat16)
    code_one, scale_one = requantize(first)
    code_two, scale_two = requantize(second)
    return (updated, code_one, scale_one, code_two, scale_two)

def reference(tokens, cotangent, gate_up, down_weight, first_code, first_scale, second_code, second_scale):
    total = tokens.shape[0]
    group = total // N_DP
    width = gate_up.shape[2] // N_TENSOR
    pre = jnp.einsum('td,kdf->tkf', tokens.astype(jnp.float32), gate_up.astype(jnp.float32))
    gate = pre[:, 0]
    upper = pre[:, 1]
    hidden_grad = jnp.dot(cotangent, down_weight.T, preferred_element_type=jnp.float32)
    sigma = jax.nn.sigmoid(gate)
    gate_grad = hidden_grad * upper * sigma * (1.0 + gate * (1.0 - sigma))
    upper_grad = hidden_grad * gate * sigma
    pre_grad = jnp.stack([gate_grad, upper_grad], axis=1).astype(jnp.bfloat16)
    summed = jnp.zeros(gate_up.shape, jnp.float32)
    for member in range(N_DP):
        rows = tokens[member * group:(member + 1) * group].astype(jnp.float32)
        grads = pre_grad[member * group:(member + 1) * group].astype(jnp.float32)
        partial_value = jnp.einsum('td,tkf->kdf', rows, grads).astype(jnp.bfloat16)
        partial_value = lax.optimization_barrier(partial_value)
        summed = summed + partial_value.astype(jnp.float32)
    grad = summed / jnp.sqrt(jnp.float32(total))
    input_sum = jnp.zeros(tokens.shape, jnp.float32)
    for member in range(N_TENSOR):
        grads = pre_grad[:, :, member * width:(member + 1) * width].astype(jnp.float32)
        weights = gate_up[:, :, member * width:(member + 1) * width].astype(jnp.float32)
        partial_value = jnp.einsum('tkf,kdf->td', grads, weights).astype(jnp.bfloat16)
        partial_value = lax.optimization_barrier(partial_value)
        input_sum = input_sum + partial_value.astype(jnp.float32)
    input_grad = input_sum.astype(jnp.bfloat16)
    updated, code_one, scale_one, code_two, scale_two = optimizer(gate_up, first_code, first_scale, second_code, second_scale, grad)
    return (input_grad, updated, code_one, scale_one, code_two, scale_two)
```

```python
import functools

import jax
import jax.numpy as jnp
from jax import lax
from jax.experimental import pallas as pl
from jax.experimental.pallas import tpu as pltpu
from jax.sharding import PartitionSpec as P

learning_rate = 0.003
beta_first = 0.9
beta_second = 0.95
f32 = jnp.float32
bf16 = jnp.bfloat16


def swap(value, mask):
    return lax.ppermute(value, "dp", [(p, p ^ mask) for p in range(lax.axis_size("dp"))])


def pair(value):
    return lax.ppermute(value, "tensor", [(p, p ^ 1) for p in range(lax.axis_size("tensor"))])


def ring(value):
    size = lax.axis_size("tensor")
    return lax.ppermute(value, "tensor", [(p, (p + 2) % size) for p in range(size)])


def adam_kernel(parts, total_tokens, *refs):
    token_refs = refs[:parts]
    grad_refs = refs[parts : 2 * parts]
    weight_ref, first_ref, first_scale_ref, second_ref, second_scale_ref = refs[2 * parts : 2 * parts + 5]
    out_weight, out_first, out_first_scale, out_second, out_second_scale, total = refs[-6:]
    value = None
    for token_ref, grad_ref in zip(token_refs, grad_refs):
        term = jnp.dot(token_ref[...], grad_ref[0], preferred_element_type=f32)
        value = term if value is None else value + term
    total[...] = value
    rows, columns = total.shape
    step = 8
    inverse = 1.0 / (float(total_tokens) ** 0.5)

    def body(at, carry):
        span = pl.ds(pl.multiple_of(at * step * 16, step * 16), step * 16)
        blocks = pl.ds(pl.multiple_of(at * step, step), step)
        shape = (step, 16, columns)
        grad = (total[span, :] * inverse).reshape(shape)
        first = first_ref[0, span, :].astype(f32).reshape(shape) * first_scale_ref[0, blocks][:, None, :]
        second = second_ref[0, span, :].astype(f32).reshape(shape) * second_scale_ref[0, blocks][:, None, :]
        first = beta_first * first + (1.0 - beta_first) * grad
        second = beta_second * second + (1.0 - beta_second) * grad * grad
        weight = weight_ref[0, span, :].astype(f32).reshape(shape)
        weight = weight - learning_rate * first / (jnp.sqrt(second) + 1e-08)
        out_weight[0, span, :] = weight.reshape(step * 16, columns).astype(bf16)
        for state, code_ref, scale_ref in ((first, out_first, out_first_scale), (second, out_second, out_second_scale)):
            peak = jnp.max(jnp.abs(state), axis=1)
            peaks = []
            for c in range(columns // 128):
                top = jnp.max(peak[:, c * 128 : (c + 1) * 128], axis=1, keepdims=True) + 1e-06
                peaks.append(jnp.broadcast_to(top, (step, 128)))
            peak = jnp.concatenate(peaks, axis=1)
            scale_ref[0, blocks] = peak
            code = state * (1.0 / peak)[:, None, :]
            code_ref[0, span, :] = code.reshape(step * 16, columns).astype(bf16)
        return carry

    lax.fori_loop(0, rows // (step * 16), body, 0)


def adam(parts, weight, first, first_scale, second, second_scale, outs, chunk, width, total_tokens):
    rows = weight.shape[1]
    tile = min(512, rows)
    n = len(parts)
    big = pl.BlockSpec((1, tile, width), lambda k, r: (k, r, chunk))
    scale = pl.BlockSpec((1, tile // 16, width), lambda k, r: (k, r, chunk))
    specs = [pl.BlockSpec((tile, t.shape[1]), lambda k, r: (r, 0)) for t, _, _ in parts]
    for _, g, at in parts:
        specs.append(pl.BlockSpec((1, g.shape[1], width), lambda k, r, at=at: (k, 0, at)))
    specs += [big, big, scale, big, scale]
    operands = [t for t, _, _ in parts] + [g for _, g, _ in parts] + [weight, first, first_scale, second, second_scale]
    aliases = {}
    if outs is not None:
        aliases = {len(operands) + i: i for i in range(5)}
        specs += [pl.BlockSpec(memory_space=pl.ANY)] * 5
        operands += list(outs)
    elements = 2 * rows * width
    return pl.pallas_call(
        functools.partial(adam_kernel, n, total_tokens),
        grid=(2, rows // tile),
        in_specs=specs,
        out_specs=[big, big, scale, big, scale],
        out_shape=[
            jax.ShapeDtypeStruct(weight.shape, bf16),
            jax.ShapeDtypeStruct(weight.shape, bf16),
            jax.ShapeDtypeStruct(first_scale.shape, f32),
            jax.ShapeDtypeStruct(weight.shape, bf16),
            jax.ShapeDtypeStruct(first_scale.shape, f32),
        ],
        input_output_aliases=aliases,
        scratch_shapes=[pltpu.VMEM((tile, width), f32)],
        compiler_params=pltpu.CompilerParams(vmem_limit_bytes=32 << 20),
        cost_estimate=pl.CostEstimate(
            flops=2 * elements * sum(t.shape[1] for t, _, _ in parts) + 40 * elements,
            bytes_accessed=12 * elements,
            transcendentals=2 * elements,
        ),
        name="weight_step",
    )(*operands)


def shards(tokens, cotangent, gate_up, down_weight, first_code, first_scale, second_code, second_scale):
    groups = lax.axis_size("dp")
    bits = groups.bit_length() - 1
    chips = lax.axis_size("tensor") // 2
    me = lax.axis_index("dp")
    own, depth = tokens.shape
    rows, units = gate_up.shape[1:]
    width = 256 if units % 256 == 0 else 128
    chunks = units // width
    total_tokens = own * groups * lax.axis_size("tensor")
    orders = [list(range(bits)), list(reversed(range(bits)))]

    blocks = tokens.reshape(own, groups, rows)
    slots = []
    for s in range(groups):
        block = lax.dynamic_index_in_dim(blocks, me ^ s, 1, keepdims=False)
        slots.append(swap(block, s) if s else block)
    block = jnp.stack(slots)
    token_blocks = []
    grad_blocks = []
    cot = cotangent
    for k in range(chips):
        if k:
            block = ring(block)
        token_blocks.append(jnp.concatenate([block, pair(block)], axis=1))
    for k in range(chips):
        if k:
            cot = ring(cot)
        grad_blocks.append(jnp.concatenate([cot, pair(cot)], axis=0))

    every = tuple(range(chips))
    lead = max(1, (chunks * 4) // 7)
    plan = [((0,), 0, lead)]
    for c in range(lead):
        plan.append((every[1:], c, c + 1))
    for c in range(lead, chunks):
        plan.append((every, c, c + 1))

    cache = {}

    def rows_of(ks):
        if ks not in cache:
            t = jnp.concatenate([token_blocks[k] for k in ks], axis=1)
            c = jnp.concatenate([grad_blocks[k] for k in ks], axis=0)
            flat = t.reshape(-1, rows)
            cache[ks] = (t, c, flat.T)
        return cache[ks]

    expand = lambda scale: jnp.repeat(scale, 128, axis=2)
    first_wide = expand(first_scale)
    second_wide = expand(second_scale)

    def forward(ks, c0, c1):
        t, c, _ = rows_of(ks)
        n = t.shape[1]
        lo, hi = c0 * width, c1 * width
        pre = []
        for k in range(2):
            w = gate_up[k, :, lo:hi]
            dot = lambda pick: jnp.dot(
                jnp.concatenate([t[s] for s in pick], axis=0), w, preferred_element_type=f32
            ).reshape(len(pick), n, hi - lo)
            held = {}
            active = list(range(groups))
            got = {s: [] for s in active}
            for b in orders[k]:
                mask = 1 << b
                send = [s for s in active if s & mask]
                active = [s for s in active if not s & mask]
                out = dot(send)
                for at, s in enumerate(send):
                    for extra in got[s]:
                        out = out.at[at].add(extra.astype(f32)) if len(send) > 1 else out + extra.astype(f32)[None]
                back = swap(out.astype(bf16), mask)
                for at, s in enumerate(send):
                    got[s ^ mask].append(back[at])
            value = dot([0])[0]
            for extra in got[0]:
                value = value + extra.astype(f32)
            pre.append(value)
        gate, upper = pre
        hidden = lax.dot_general(
            c, down_weight[lo:hi], (((1,), (1,)), ((), ())), preferred_element_type=f32
        )
        sigma = jax.nn.sigmoid(gate)
        grads = (
            (hidden * upper * sigma * (1.0 + gate * (1.0 - sigma))).astype(bf16),
            (hidden * gate * sigma).astype(bf16),
        )
        full = []
        for k in range(2):
            held = {0: grads[k]}
            for b in reversed(orders[k]):
                mask = 1 << b
                keys = sorted(held)
                back = swap(jnp.stack([held[s] for s in keys]), mask)
                for at, s in enumerate(keys):
                    held[s ^ mask] = back[at]
            full.append(jnp.concatenate([held[s] for s in range(groups)], axis=0))
        return jnp.stack(full)

    results = [(ks, c0, c1, forward(ks, c0, c1)) for ks, c0, c1 in plan]

    sums = {}
    for ks, c0, c1, g in results:
        term = jnp.einsum(
            "ktf,kdf->td", g, gate_up[:, :, c0 * width : c1 * width], preferred_element_type=f32
        )
        sums[ks] = term if ks not in sums else sums[ks] + term
    partial = [None] * chips
    for ks, value in sums.items():
        value = value.reshape(groups, len(ks), 2, own, rows)
        for at, k in enumerate(ks):
            part = value[:, at]
            partial[k] = part if partial[k] is None else partial[k] + part
    moving = None
    for k in every[1:] + (0,):
        mine = partial[k][:, 0] + pair(partial[k][:, 1].astype(bf16)).astype(f32)
        if moving is not None:
            mine = mine + ring(moving).astype(f32)
        moving = mine.astype(bf16)
    final = [moving[0]] + [swap(moving[s], s) for s in range(1, groups)]
    final = jnp.stack(final)
    final = jnp.stack([lax.dynamic_index_in_dim(final, me ^ a, 0, keepdims=False) for a in range(groups)], axis=1)
    input_grad = final.reshape(own, depth)

    outs = None
    for chunk in range(chunks):
        parts = []
        for ks, c0, c1, g in results:
            if c0 <= chunk < c1:
                parts.append((rows_of(ks)[2], g, chunk - c0))
        outs = adam(
            parts, gate_up, first_code, first_wide, second_code, second_wide, outs, chunk, width, total_tokens
        )
    updated, code_one, scale_one, code_two, scale_two = outs
    return (input_grad, updated, code_one, scale_one[:, :, ::128], code_two, scale_two[:, :, ::128])


def solution(mesh):
    placed = (
        P(("dp", "tensor"), None),
        P(("dp", "tensor"), None),
        P(None, "dp", "tensor"),
        P("tensor", None),
        P(None, "dp", "tensor"),
        P(None, "dp", "tensor"),
        P(None, "dp", "tensor"),
        P(None, "dp", "tensor"),
    )
    return jax.shard_map(
        shards,
        mesh=mesh,
        in_specs=placed,
        out_specs=(
            P(("dp", "tensor"), None),
            P(None, "dp", "tensor"),
            P(None, "dp", "tensor"),
            P(None, "dp", "tensor"),
            P(None, "dp", "tensor"),
            P(None, "dp", "tensor"),
        ),
        check_vma=False,
    )
```

```python
import functools

import jax
import jax.numpy as jnp
from jax import lax
from jax.experimental import pallas as pl
from jax.experimental.pallas import tpu as pltpu
from jax.sharding import PartitionSpec as P

learning_rate = 0.003
beta_first = 0.9
beta_second = 0.95
f32 = jnp.float32
bf16 = jnp.bfloat16


def swap(value, mask):
    return lax.ppermute(value, "dp", [(p, p ^ mask) for p in range(lax.axis_size("dp"))])


def pair(value):
    return lax.ppermute(value, "tensor", [(p, p ^ 1) for p in range(lax.axis_size("tensor"))])


def ring(value):
    size = lax.axis_size("tensor")
    return lax.ppermute(value, "tensor", [(p, (p + 2) % size) for p in range(size)])


class Chain:
    def __init__(self):
        self.tokens = []

    def add(self, value):
        self.tokens.append(value)

    def call(self, kernel, in_specs, operands, out_specs, out_shape, name, vmem, flops, read, scratch=(), aliases=None):
        inputs, held, outputs = len(operands), len(self.tokens), len(out_shape)

        def body(*refs):
            kernel(*refs[:inputs], *refs[inputs + held : inputs + held + outputs], *refs[inputs + held + outputs + 1 :])

        anywhere = pl.BlockSpec(memory_space=pl.ANY)
        outs = pl.pallas_call(
            body,
            in_specs=list(in_specs) + [anywhere] * held,
            out_specs=list(out_specs) + [anywhere],
            out_shape=list(out_shape) + [jax.ShapeDtypeStruct((8, 128), f32)],
            input_output_aliases=aliases or {},
            scratch_shapes=list(scratch),
            compiler_params=pltpu.CompilerParams(vmem_limit_bytes=vmem << 20),
            cost_estimate=pl.CostEstimate(flops=flops, bytes_accessed=read, transcendentals=0),
            name=name,
        )(*operands, *self.tokens)
        self.tokens = [outs[-1]]
        return outs[:-1]


in_vmem = pl.BlockSpec(memory_space=pltpu.VMEM)
in_hbm = pl.BlockSpec(memory_space=pltpu.HBM)


def weight_kernel(parts, total_tokens, c0, columns, tile, *refs):
    token_refs = refs[:parts]
    grad_refs = [ref for ref in refs[parts : 2 * parts]]
    sources = refs[2 * parts : 2 * parts + 5]
    targets = refs[-6:-1]
    total = refs[-1]
    starts = [at for at, _ in total_tokens[1]]
    first_gain = (1.0 - beta_first) / float(total_tokens[0]) ** 0.5
    second_gain = (1.0 - beta_second) / float(total_tokens[0])
    group = 8
    rows = sources[0].shape[1]
    lanes = 256 if columns % 256 == 0 else 128

    def work(weight_ref, first_ref, first_scale_ref, second_ref, second_scale_ref, *outs):
        out_weight, out_first, out_first_scale, out_second, out_second_scale = outs
        k, r = pl.program_id(0), pl.program_id(1)
        value = None
        for token_ref, grad_ref, start in zip(token_refs, grad_refs, starts):
            term = lax.dot_general(
                token_ref[:, pl.ds(pl.multiple_of(r * tile, tile), tile)],
                grad_ref[k, :, pl.ds(start, columns)],
                (((0,), (0,)), ((), ())),
                preferred_element_type=f32,
            )
            value = term if value is None else value + term
        total[...] = value

        def body(at, carry):
            base = pl.multiple_of(at * group, group)
            for lane in range(0, columns, lanes):
                side = pl.ds(lane, lanes)
                scale_one = first_scale_ref[0, pl.ds(base, group), side] * beta_first
                scale_two = second_scale_ref[0, pl.ds(base, group), side] * beta_second
                tops_one, tops_two = [], []
                for b in range(group):
                    span = pl.ds(pl.multiple_of(at * group * 16, group * 16) + b * 16, 16)
                    grad = total[span, side]
                    first = first_ref[0, span, side].astype(f32) * scale_one[b : b + 1] + first_gain * grad
                    second = second_ref[0, span, side].astype(f32) * scale_two[b : b + 1] + second_gain * (grad * grad)
                    root = second * lax.rsqrt(second)
                    step = (learning_rate * first) * pl.reciprocal(root + 1e-08, approx=True)
                    out_weight[0, span, side] = (weight_ref[0, span, side].astype(f32) - step).astype(bf16)
                    for state, size, code_ref, tops in (
                        (first, jnp.abs(first), out_first, tops_one),
                        (second, second, out_second, tops_two),
                    ):
                        peak = jnp.max(size, axis=0, keepdims=True)
                        wide = []
                        for c in range(0, lanes, 128):
                            top = jnp.max(peak[:, c : c + 128], axis=1, keepdims=True) + 1e-06
                            wide.append(jnp.broadcast_to(top, (1, 128)))
                        peak = jnp.concatenate(wide, axis=1)
                        tops.append(peak)
                        inverse = pl.reciprocal(peak, approx=True)
                        inverse = inverse * (2.0 - peak * inverse)
                        code_ref[0, span, side] = (state * inverse).astype(bf16)
                out_first_scale[0, pl.ds(base, group), side] = jnp.concatenate(tops_one, axis=0)
                out_second_scale[0, pl.ds(base, group), side] = jnp.concatenate(tops_two, axis=0)
            return carry

        lax.fori_loop(0, tile // (group * 16), body, 0)

    big = pl.BlockSpec((1, tile, columns), lambda k, r: (k, r, 0))
    scale = pl.BlockSpec((1, tile // 16, columns), lambda k, r: (k, r, 0))
    specs = [big, big, scale, big, scale]
    cut = lambda ref: ref.at[:, :, pl.ds(c0, columns)]
    pltpu.emit_pipeline(work, grid=(2, rows // tile), in_specs=specs, out_specs=specs)(
        *[cut(ref) for ref in sources], *[cut(ref) for ref in targets]
    )


def weight_step(chain, parts, weight, first, first_scale, second, second_scale, outs, c0, columns, total_tokens):
    rows = weight.shape[1]
    tile = min(512, rows)
    n = len(parts)
    operands = [t for t, _, _ in parts] + [g for _, g, _ in parts] + [weight, first, first_scale, second, second_scale]
    specs = [in_vmem] * (2 * n) + [in_hbm] * 5
    aliases = {}
    if outs is not None:
        aliases = {len(operands) + i: i for i in range(5)}
        specs += [in_hbm] * 5
        operands += list(outs)
    elements = 2 * rows * columns
    kernel = functools.partial(weight_kernel, n, (total_tokens, [(at, 0) for _, _, at in parts]), c0, columns, tile)
    return chain.call(
        kernel,
        specs,
        operands,
        [in_hbm] * 5,
        [jax.ShapeDtypeStruct(v.shape, v.dtype) for v in (weight, first, first_scale, second, second_scale)],
        "weight_step",
        20,
        2 * elements * sum(t.shape[0] for t, _, _ in parts) + 40 * elements,
        12 * elements,
        scratch=[pltpu.VMEM((tile, columns), f32)],
        aliases=aliases,
    )


def pre_kernel(c0, count, width, token_ref, weight_ref, send_ref, keep_ref):
    n = token_ref.shape[0] // 4
    depth = weight_ref.shape[1]

    def work(block):
        k, c = pl.program_id(0), pl.program_id(1)
        value = jnp.dot(token_ref[...], block[0], preferred_element_type=f32)
        span = pl.ds(pl.multiple_of(c * n, n), n)
        send_ref[k, span] = value[3 * n :].astype(bf16)
        for slot in range(3):
            keep_ref[slot, k, span] = value[slot * n : (slot + 1) * n]

    spec = pl.BlockSpec((1, depth, width), lambda k, c: (k, 0, c))
    pltpu.emit_pipeline(work, grid=(2, count), in_specs=[spec])(weight_ref.at[:, :, pl.ds(c0 * width, count * width)])


def partial_pre(chain, tokens, weight, c0, c1, width):
    rows, depth = tokens.shape
    n = rows // 4
    count = c1 - c0
    return chain.call(
        functools.partial(pre_kernel, c0, count, width),
        [in_vmem, in_hbm],
        [tokens, weight],
        [in_vmem, in_vmem],
        [jax.ShapeDtypeStruct((2, count * n, width), bf16), jax.ShapeDtypeStruct((3, 2, count * n, width), f32)],
        "partial_pre",
        8,
        4 * rows * depth * count * width,
        4 * depth * count * width,
    )


def hidden_kernel(c0, count, width, grad_ref, down_ref, out_ref):
    n, depth = grad_ref.shape

    def work(block):
        c = pl.program_id(0)
        out_ref[pl.ds(pl.multiple_of(c * n, n), n)] = lax.dot_general(
            grad_ref[...], block[...], (((1,), (1,)), ((), ())), preferred_element_type=f32
        )

    spec = pl.BlockSpec((width, depth), lambda c: (c, 0))
    pltpu.emit_pipeline(work, grid=(count,), in_specs=[spec])(down_ref.at[pl.ds(c0 * width, count * width)])


def hidden_grad(chain, cot, down, c0, c1, width):
    rows, depth = cot.shape
    count = c1 - c0
    (out,) = chain.call(
        functools.partial(hidden_kernel, c0, count, width),
        [in_vmem, in_hbm],
        [cot, down],
        [in_vmem],
        [jax.ShapeDtypeStruct((count * rows, width), f32)],
        "hidden_grad",
        8,
        2 * rows * depth * count * width,
        2 * depth * count * width,
    )
    return out


def step_kernel(has, offsets, *refs):
    refs = list(refs)
    take = lambda: refs.pop(0)
    counts = {0: 1, 1: 3, 2: 4, 3: 2}
    inputs = {s: [take() for _ in range(counts[s])] for s in has}
    out_x, out_y = take(), take()
    if 0 in has:
        (send,) = inputs[0]
        at, size, _ = offsets[0]
        out_x[pl.ds(at, size)] = send[0]
        out_y[pl.ds(at, size)] = send[1]
    if 1 in has:
        keep, got_x, got_y = inputs[1]
        at, size, start = offsets[1]
        span = pl.ds(start, size)
        out_x[pl.ds(at, size)] = keep[1, 0].astype(bf16)
        out_x[pl.ds(at + size, size)] = (keep[1, 1] + got_y[span].astype(f32)).astype(bf16)
        out_y[pl.ds(at, size)] = (keep[2, 0] + got_x[span].astype(f32)).astype(bf16)
        out_y[pl.ds(at + size, size)] = keep[2, 1].astype(bf16)
    if 2 in has:
        keep, hidden, got_x, got_y = inputs[2]
        at, size, start = offsets[2]
        own = take()
        gate = keep[0, 0] + got_x[pl.ds(start, size)].astype(f32) + got_y[pl.ds(start, size)].astype(f32)
        upper = (
            keep[0, 1] + got_x[pl.ds(start + size, size)].astype(f32) + got_y[pl.ds(start + size, size)].astype(f32)
        )
        grad = hidden[...]
        sigma = jax.nn.sigmoid(gate)
        first = (grad * upper * sigma * (1.0 + gate * (1.0 - sigma))).astype(bf16)
        second = (grad * gate * sigma).astype(bf16)
        own[0] = first
        own[1] = second
        for out in (out_x, out_y):
            out[pl.ds(at, size)] = first
            out[pl.ds(at + size, size)] = second
    if 3 in has:
        got_x, got_y = inputs[3]
        at, size, start = offsets[3]
        out_x[pl.ds(at, size)] = got_y[pl.ds(start, size)]
        out_y[pl.ds(at, size)] = got_x[pl.ds(start + size, size)]


def gather_kernel(offset_one, offset_two, size, n, own, x_one, y_one, x_two, y_two, out):
    width = own.shape[2]
    for c in range(size // n):
        columns = pl.ds(c * width, width)
        rows = c * n
        for k in range(2):
            at = offset_one + k * size + rows
            out[k, pl.ds(0, n), columns] = own[k, pl.ds(rows, n)]
            out[k, pl.ds(n, n), columns] = x_one[pl.ds(at, n)]
            out[k, pl.ds(2 * n, n), columns] = y_one[pl.ds(at, n)]
        out[0, pl.ds(3 * n, n), columns] = x_two[pl.ds(offset_two + rows, n)]
        out[1, pl.ds(3 * n, n), columns] = y_two[pl.ds(offset_two + rows, n)]


class Exchange:
    def __init__(self, chain, units, lag, own_rows, width):
        self.chain, self.units, self.lag, self.width, self.own_rows = chain, units, lag, width, own_rows
        self.sends, self.keeps, self.hidden = {}, {}, {}
        self.got, self.place, self.own = {}, {}, {}

    def rows_in(self, u):
        return 2 * self.own_rows * len(self.units[u][0])

    def size_of(self, u):
        return (self.units[u][2] - self.units[u][1]) * self.rows_in(u)

    def stages(self, m):
        return {s: m - s * self.lag for s in range(4) if (m - s * self.lag) in self.units}

    def step(self, m):
        stages, lag = self.stages(m), self.lag
        pieces = (1, 2, 2, 1)
        offsets, at, operands = {}, 0, []
        for s, u in stages.items():
            size = self.size_of(u)
            offsets[s] = (at, size, self.place[u, s - 1] if s else 0)
            self.place[u, s] = at
            at += pieces[s] * size
            if s == 0:
                operands += [self.sends[u]]
            elif s == 1:
                operands += [self.keeps[u], *self.got[m - lag]]
            elif s == 2:
                operands += [self.keeps[u], self.hidden[u], *self.got[m - lag]]
            else:
                operands += [*self.got[m - lag]]
        shapes = [jax.ShapeDtypeStruct((at, self.width), bf16)] * 2
        if 2 in stages:
            shapes.append(jax.ShapeDtypeStruct((2, self.size_of(stages[2]), self.width), bf16))
        outs = self.chain.call(
            functools.partial(step_kernel, tuple(stages), offsets),
            [in_vmem] * len(operands),
            operands,
            [in_vmem] * len(shapes),
            shapes,
            "exchange_step",
            4,
            8 * at * self.width,
            8 * at * self.width,
        )
        self.got[m] = (swap(outs[0], 1), swap(outs[1], 2))
        if 2 in stages:
            self.own[stages[2]] = outs[2]

    def gather(self, u):
        n, columns = self.rows_in(u), (self.units[u][2] - self.units[u][1]) * self.width
        (out,) = self.chain.call(
            functools.partial(gather_kernel, self.place[u, 2], self.place[u, 3], self.size_of(u), n),
            [in_vmem] * 5,
            [self.own[u], *self.got[u + 2 * self.lag], *self.got[u + 3 * self.lag]],
            [in_vmem],
            [jax.ShapeDtypeStruct((2, 4 * n, columns), bf16)],
            "pre_grad",
            4,
            0,
            16 * n * columns,
        )
        return out


def shards(tokens, cotangent, gate_up, down_weight, first_code, first_scale, second_code, second_scale):
    groups = lax.axis_size("dp")
    bits = groups.bit_length() - 1
    chips = lax.axis_size("tensor") // 2
    me = lax.axis_index("dp")
    own, depth = tokens.shape
    rows, units = gate_up.shape[1:]
    width = 256 if units % 256 == 0 else 128
    chunks = units // width
    total_tokens = own * groups * lax.axis_size("tensor")
    orders = [list(range(bits)), list(reversed(range(bits)))]
    every = tuple(range(chips))
    rest = every[1:]
    staged = groups == 4 and chips == 4 and chunks >= 4

    blocks = tokens.reshape(own, groups, rows)
    slots = []
    for s in range(groups):
        block = lax.dynamic_index_in_dim(blocks, me ^ s, 1, keepdims=False)
        slots.append(swap(block, s) if s else block)
    block = jnp.stack(slots)
    def around(value, axis):
        moved, found = value, []
        for _ in rest:
            moved = ring(moved)
            found.append(moved)
        result = [jnp.concatenate([value, pair(value)], axis=axis)]
        if found:
            other = pair(jnp.stack(found))
            result += [jnp.concatenate([v, other[at]], axis=axis) for at, v in enumerate(found)]
        return result

    token_blocks = around(block, 1)
    grad_blocks = around(cotangent, 0)

    if staged:
        last = chunks - max(1, (chunks * 2) // 7)
        plan = {0: ((0,), 0, last)}
        at = 4
        for c in range(0, last, 2):
            plan[at] = (rest, c, min(c + 2, last))
            at += 1
        plan[at] = (every[1:3], last, chunks)
        plan[at + 1] = ((every[3], 0), last, chunks)
    else:
        plan = {c: (every, c, c + 1) for c in range(chunks)}

    cache = {}

    def rows_of(ks):
        if ks not in cache:
            t = jnp.concatenate([token_blocks[k] for k in ks], axis=1)
            c = jnp.concatenate([grad_blocks[k] for k in ks], axis=0)
            cache[ks] = (t, c, t.reshape(-1, rows))
        return cache[ks]

    expand = lambda scale: jnp.repeat(scale, 128, axis=2)
    first_wide = expand(first_scale)
    second_wide = expand(second_scale)

    def forward(ks, c0, c1):
        t, c, _ = rows_of(ks)
        n = t.shape[1]
        lo, hi = c0 * width, c1 * width
        pre = []
        for k in range(2):
            w = gate_up[k, :, lo:hi]
            dot = lambda pick: jnp.dot(
                jnp.concatenate([t[s] for s in pick], axis=0), w, preferred_element_type=f32
            ).reshape(len(pick), n, hi - lo)
            active = list(range(groups))
            got = {s: [] for s in active}
            for b in orders[k]:
                mask = 1 << b
                send = [s for s in active if s & mask]
                active = [s for s in active if not s & mask]
                out = dot(send)
                for at, s in enumerate(send):
                    for extra in got[s]:
                        out = out.at[at].add(extra.astype(f32)) if len(send) > 1 else out + extra.astype(f32)[None]
                back = swap(out.astype(bf16), mask)
                for at, s in enumerate(send):
                    got[s ^ mask].append(back[at])
            value = dot([0])[0]
            for extra in got[0]:
                value = value + extra.astype(f32)
            pre.append(value)
        gate, upper = pre
        hidden = lax.dot_general(
            c, down_weight[lo:hi], (((1,), (1,)), ((), ())), preferred_element_type=f32
        )
        sigma = jax.nn.sigmoid(gate)
        grads = (
            (hidden * upper * sigma * (1.0 + gate * (1.0 - sigma))).astype(bf16),
            (hidden * gate * sigma).astype(bf16),
        )
        full = []
        for k in range(2):
            held = {0: grads[k]}
            for b in reversed(orders[k]):
                mask = 1 << b
                keys = sorted(held)
                back = swap(jnp.stack([held[s] for s in keys]), mask)
                for at, s in enumerate(keys):
                    held[s ^ mask] = back[at]
            full.append(jnp.concatenate([held[s] for s in range(groups)], axis=0))
        return jnp.stack(full)

    product = lambda g, c0, c1: jnp.einsum(
        "ktf,kdf->td", g, gate_up[:, :, c0 * width : c1 * width], preferred_element_type=f32
    )
    sums = {}

    def add_input_grad(u, g):
        ks, c0, c1 = plan[u]
        term = product(g, c0, c1)
        sums[ks] = term if ks not in sums else sums[ks] + term
        return sums[ks]

    def split(ks):
        value = sums[ks].reshape(groups, len(ks), 2, own, rows)
        return {k: value[:, at] for at, k in enumerate(ks)}

    grads = {}
    if staged:
        chain = Chain()
        lag = 2
        exchange = Exchange(chain, plan, lag, own, width)
        steps = [m for m in range(max(plan) + 3 * lag + 1) if exchange.stages(m)]
        sources = (gate_up, first_code, first_wide, second_code, second_wide)
        result = [None]

        def start(u):
            exchange.sends[u], exchange.keeps[u] = partial_pre(chain, rows_of(plan[u][0])[2], gate_up, *plan[u][1:], width)

        def hidden(u):
            exchange.hidden[u] = hidden_grad(chain, rows_of(plan[u][0])[1], down_weight, *plan[u][1:], width)

        def finish(u):
            grads[u] = exchange.gather(u)

        def inputs(u):
            chain.add(add_input_grad(u, grads[u]))

        def update(c0, c1):
            parts = []
            for u, (ks, a, b) in plan.items():
                if a <= c0 and c1 <= b:
                    parts.append((rows_of(ks)[2], grads[u], (c0 - a) * width))
            result[0] = weight_step(
                chain, parts, *sources, result[0], c0 * width, (c1 - c0) * width, total_tokens
            )

        hidden(0)
        start(0)
        spans = [p[1:] for p in plan.values() if p[0] == rest]
        updated_spans = []
        for place, m in enumerate(steps):
            exchange.step(m)
            if place + 1 < len(steps):
                after = steps[place + 1]
                if after in plan:
                    start(after)
                if after - 2 * lag in plan and after != 2 * lag:
                    hidden(after - 2 * lag)
            if m - 4 * lag in plan:
                finish(m - 4 * lag)
                inputs(m - 4 * lag)
                if plan[m - 4 * lag][1:] in spans[:1]:
                    update(*spans[0])
        left = [u for u in plan if u not in grads]
        for u in left:
            finish(u)
            inputs(u)
            if u == left[-2]:
                for span in spans[1:-1]:
                    update(*span)
        for span in spans[max(1, len(spans) - 1) :]:
            update(*span)
        update(last, chunks)
        outs = result[0]
    else:
        for u, unit in plan.items():
            grads[u] = forward(*unit)
            add_input_grad(u, grads[u])

    partial = [None] * chips
    for ks in sums:
        for k, part in split(ks).items():
            partial[k] = part if partial[k] is None else partial[k] + part
    order = rest + (0,)
    mine = {}
    for at in range(0, chips, 2):
        ks = order[at : at + 2]
        theirs = pair(jnp.stack([partial[k][:, 1] for k in ks]).astype(bf16))
        for spot, k in enumerate(ks):
            mine[k] = partial[k][:, 0] + theirs[spot].astype(f32)
    moving = None
    for k in order:
        value = mine[k]
        if moving is not None:
            value = value + ring(moving).astype(f32)
        moving = value.astype(bf16)
    final = [moving[0]] + [swap(moving[s], s) for s in range(1, groups)]
    final = jnp.stack(final)
    final = jnp.stack([lax.dynamic_index_in_dim(final, me ^ a, 0, keepdims=False) for a in range(groups)], axis=1)
    input_grad = final.reshape(own, depth)

    if not staged:
        chain, outs = Chain(), None
        for c, (ks, c0, c1) in plan.items():
            outs = weight_step(
                chain,
                [(rows_of(ks)[2], grads[c], 0)],
                gate_up,
                first_code,
                first_wide,
                second_code,
                second_wide,
                outs,
                c0 * width,
                (c1 - c0) * width,
                total_tokens,
            )
    updated, code_one, scale_one, code_two, scale_two = outs
    return (input_grad, updated, code_one, scale_one[:, :, ::128], code_two, scale_two[:, :, ::128])


def solution(mesh):
    placed = (
        P(("dp", "tensor"), None),
        P(("dp", "tensor"), None),
        P(None, "dp", "tensor"),
        P("tensor", None),
        P(None, "dp", "tensor"),
        P(None, "dp", "tensor"),
        P(None, "dp", "tensor"),
        P(None, "dp", "tensor"),
    )
    return jax.shard_map(
        shards,
        mesh=mesh,
        in_specs=placed,
        out_specs=(
            P(("dp", "tensor"), None),
            P(None, "dp", "tensor"),
            P(None, "dp", "tensor"),
            P(None, "dp", "tensor"),
            P(None, "dp", "tensor"),
            P(None, "dp", "tensor"),
        ),
        check_vma=False,
    )
```

```python
import functools

import jax
import jax.numpy as jnp
from jax import lax
from jax.experimental import pallas as pl
from jax.experimental.pallas import tpu as pltpu
from jax.sharding import PartitionSpec as P

learning_rate = 0.003
beta_first = 0.9
beta_second = 0.95
f32 = jnp.float32
bf16 = jnp.bfloat16
in_vmem = pl.BlockSpec(memory_space=pltpu.VMEM)
in_hbm = pl.BlockSpec(memory_space=pltpu.HBM)


def swap(value, mask):
    return lax.ppermute(value, "dp", [(p, p ^ mask) for p in range(lax.axis_size("dp"))])


def back(value, distance):
    size = lax.axis_size("tensor")
    return lax.ppermute(value, "tensor", [(p, (p - 2 * distance) % size) for p in range(size)])


def onward(value, distance):
    return back(value, -distance)


def pair(value):
    return lax.ppermute(value, "tensor", [(p, p ^ 1) for p in range(lax.axis_size("tensor"))])


def split_kernel(groups, rows, me_ref, tokens_ref, *outs):
    for s in range(groups):
        at = pl.multiple_of((me_ref[0] ^ s) * rows, 128)
        outs[s][...] = tokens_ref[:, pl.ds(at, rows)]


def split_columns(tokens, groups, me):
    own, depth = tokens.shape
    rows = depth // groups
    return pl.pallas_call(
        functools.partial(split_kernel, groups, rows),
        in_specs=[pl.BlockSpec(memory_space=pltpu.SMEM), in_vmem],
        out_specs=[in_vmem] * groups,
        out_shape=[jax.ShapeDtypeStruct((own, rows), bf16)] * groups,
        compiler_params=pltpu.CompilerParams(vmem_limit_bytes=4 << 20),
        name="split_columns",
    )(jnp.reshape(me, (1,)).astype(jnp.int32), tokens)


def hold_kernel(value_ref, *refs):
    refs[-1][...] = value_ref[...]


def hold_until(value, *others):
    return pl.pallas_call(
        hold_kernel,
        in_specs=[in_vmem] + [pl.BlockSpec(memory_space=pl.ANY)] * len(others),
        out_specs=in_vmem,
        out_shape=jax.ShapeDtypeStruct(value.shape, value.dtype),
        compiler_params=pltpu.CompilerParams(vmem_limit_bytes=4 << 20),
        name="hold",
    )(value, *others)


def pack_kernel(cuts, axis, *refs):
    out, at = refs[-1], 0
    for ref, (lo, hi) in zip(refs, cuts):
        if axis:
            out[:, at : at + hi - lo] = ref[:, lo:hi]
        else:
            out[at : at + hi - lo] = ref[lo:hi]
        at += hi - lo


def pack(pieces, axis, *others):
    shape = list(pieces[0][0].shape)
    shape[axis] = sum(hi - lo for _, lo, hi in pieces)
    return pl.pallas_call(
        functools.partial(pack_kernel, [p[1:] for p in pieces], axis),
        in_specs=[in_vmem] * len(pieces) + [pl.BlockSpec(memory_space=pl.ANY)] * len(others),
        out_specs=in_vmem,
        out_shape=jax.ShapeDtypeStruct(tuple(shape), pieces[0][0].dtype),
        compiler_params=pltpu.CompilerParams(vmem_limit_bytes=4 << 20),
        cost_estimate=pl.CostEstimate(flops=1, bytes_accessed=1, transcendentals=0),
        name="pack",
    )(*[p[0] for p in pieces], *others)


class Chain:
    def __init__(self):
        self.tokens = []

    def add(self, value):
        self.tokens.append(value)

    def call(self, kernel, in_specs, operands, out_specs, out_shape, name, vmem, flops, read, scratch=(), aliases=None):
        inputs, held, outputs = len(operands), len(self.tokens), len(out_shape)

        def body(*refs):
            kernel(*refs[:inputs], *refs[inputs + held : inputs + held + outputs], *refs[inputs + held + outputs + 1 :])

        anywhere = pl.BlockSpec(memory_space=pl.ANY)
        outs = pl.pallas_call(
            body,
            in_specs=list(in_specs) + [anywhere] * held,
            out_specs=list(out_specs) + [anywhere],
            out_shape=list(out_shape) + [jax.ShapeDtypeStruct((8, 128), f32)],
            input_output_aliases=aliases or {},
            scratch_shapes=list(scratch),
            compiler_params=pltpu.CompilerParams(vmem_limit_bytes=vmem << 20),
            cost_estimate=pl.CostEstimate(flops=1, bytes_accessed=1, transcendentals=0),
            name=name,
        )(*operands, *self.tokens)
        self.tokens = [outs[-1]]
        return outs[:-1]


def weight_kernel(parts, total_tokens, starts, c0, columns, tile, *refs):
    token_refs = refs[:parts]
    grad_refs = refs[parts : 2 * parts]
    weight_hbm, first_hbm, first_scale, second_hbm, second_scale = refs[2 * parts : 2 * parts + 5]
    outs_hbm = refs[-12:-9]
    first_tops, second_tops, top_table, total, rows_max, held_in, held_out, sem_in, sem_out = refs[-9:]
    first_gain = (1.0 - beta_first) / float(total_tokens) ** 0.5
    second_gain = (1.0 - beta_second) / float(total_tokens)
    group = 8
    tiles = weight_hbm.shape[1] // tile
    ins_hbm = (weight_hbm, first_hbm, second_hbm)

    def place(i):
        return i // tiles, pl.ds(pl.multiple_of(i % tiles * tile, tile), tile)

    def copies(i, out):
        k, span = place(i)
        hbm, held, sem = (outs_hbm, held_out, sem_out) if out else (ins_hbm, held_in, sem_in)
        result = []
        for a in range(3):
            far = hbm[a].at[k, span, pl.ds(c0, columns)]
            near = held.at[a, k, span]
            result.append(pltpu.make_async_copy(*((near, far) if out else (far, near)), sem.at[a, i]))
        return result

    def begin(i, carry):
        for copy in copies(i, False):
            copy.start()
        return carry

    lax.fori_loop(0, 2 * tiles, begin, 0)

    def work(i, carry):
        k, span_all = place(i)
        value = None
        for token_ref, grad_ref, start in zip(token_refs, grad_refs, starts):
            term = lax.dot_general(
                token_ref[:, span_all],
                grad_ref[k, :, pl.ds(start, columns)],
                (((0,), (0,)), ((), ())),
                preferred_element_type=f32,
            )
            value = term if value is None else value + term
        total[...] = value
        for copy in copies(i, False):
            copy.wait()

        def body(at, carry):
            base = pl.multiple_of(at * group, group)
            blocks = pl.ds(pl.multiple_of(i % tiles * (tile // 16) + base, group), group)
            tops_one, tops_two = [], []
            for lane in range(0, columns, 128):
                side = pl.ds(lane, 128)
                slot = 2 * (lane // 128)
                scale_one = first_scale[k, blocks, pl.ds(c0 + lane, 128)] * beta_first
                scale_two = second_scale[k, blocks, pl.ds(c0 + lane, 128)] * beta_second
                states = []
                for b in range(group):
                    near = pl.ds(pl.multiple_of(at * group * 16, group * 16) + b * 16, 16)
                    span = pl.ds(pl.multiple_of(i % tiles * tile + at * group * 16, group * 16) + b * 16, 16)
                    grad = total[near, side]
                    first = held_in[1, k, span, side].astype(f32) * scale_one[b : b + 1] + first_gain * grad
                    second = held_in[2, k, span, side].astype(f32) * scale_two[b : b + 1]
                    second = second + second_gain * (grad * grad)
                    root = second * lax.rsqrt(second)
                    step = (learning_rate * first) * pl.reciprocal(root + 1e-08, approx=True)
                    held_out[0, k, span, side] = (held_in[0, k, span, side].astype(f32) - step).astype(bf16)
                    size = jnp.abs(first)
                    rows_max[slot, pl.ds(b * 8, 8)] = jnp.maximum(size[:8], size[8:])
                    rows_max[slot + 1, pl.ds(b * 8, 8)] = jnp.maximum(second[:8], second[8:])
                    states.append((first, second))
                inverses = []
                for kind, tops in ((0, tops_one), (1, tops_two)):
                    peak = rows_max[slot + kind, pl.ds(0, group, stride=8)]
                    for j in range(1, 8):
                        peak = jnp.maximum(peak, rows_max[slot + kind, pl.ds(j, group, stride=8)])
                    top = jnp.max(peak, axis=1, keepdims=True) + 1e-06
                    tops.append(top)
                    wide = jnp.broadcast_to(top, (group, 128))
                    inverse = pl.reciprocal(wide, approx=True)
                    inverses.append(inverse * (2.0 - wide * inverse))
                for b, (first, second) in enumerate(states):
                    span = pl.ds(pl.multiple_of(i % tiles * tile + at * group * 16, group * 16) + b * 16, 16)
                    held_out[1, k, span, side] = (first * inverses[0][b : b + 1]).astype(bf16)
                    held_out[2, k, span, side] = (second * inverses[1][b : b + 1]).astype(bf16)
            top_table[k, blocks, pl.ds(0, columns // 128)] = jnp.concatenate(tops_one, axis=1)
            top_table[2 + k, blocks, pl.ds(0, columns // 128)] = jnp.concatenate(tops_two, axis=1)
            return carry

        lax.fori_loop(0, tile // (group * 16), body, 0)
        for copy in copies(i, True):
            copy.start()
        return carry

    lax.fori_loop(0, 2 * tiles, work, 0)

    def end(i, carry):
        for copy in copies(i, True):
            copy.wait()
        return carry

    for k in range(2):
        first_tops[:, k] = jnp.transpose(top_table[k])[: columns // 128]
        second_tops[:, k] = jnp.transpose(top_table[2 + k])[: columns // 128]
    lax.fori_loop(0, 2 * tiles, end, 0)


def weight_step(chain, vmem, parts, weight, first, first_scale, second, second_scale, outs, c0, columns, total_tokens):
    rows = weight.shape[1]
    tile = min(512, rows)
    n = len(parts)
    operands = [t for t, _, _ in parts] + [g for _, g, _ in parts] + [weight, first, first_scale, second, second_scale]
    specs = [in_vmem] * (2 * n) + [in_hbm, in_hbm, in_vmem, in_hbm, in_vmem]
    aliases = {}
    if outs is not None:
        aliases = {len(operands) + i: i for i in range(3)}
        specs += [in_hbm] * 3
        operands += list(outs)
    elements = 2 * rows * columns
    kernel = functools.partial(weight_kernel, n, total_tokens, [at for _, _, at in parts], c0, columns, tile)
    return chain.call(
        kernel,
        specs,
        operands,
        [in_hbm] * 3 + [in_vmem] * 2,
        [jax.ShapeDtypeStruct(weight.shape, bf16)] * 3
        + [jax.ShapeDtypeStruct((columns // 128, 2, rows // 16), f32)] * 2,
        "weight_step",
        vmem,
        2 * elements * sum(t.shape[0] for t, _, _ in parts) + 40 * elements,
        12 * elements,
        scratch=[
            pltpu.VMEM((4, rows // 16, 128), f32),
            pltpu.VMEM((tile, columns), f32),
            pltpu.VMEM((columns // 64, 64, 128), f32),
            pltpu.VMEM((3, 2, rows, columns), bf16),
            pltpu.VMEM((3, 2, rows, columns), bf16),
            pltpu.SemaphoreType.DMA((3, 2 * rows // tile)),
            pltpu.SemaphoreType.DMA((3, 2 * rows // tile)),
        ],
        aliases=aliases,
    )


def pre_kernel(c0, count, width, token_ref, weight_ref, send_ref, keep_ref):
    n = token_ref.shape[0] // 4
    depth = weight_ref.shape[1]

    def work(block):
        k, c = pl.program_id(0), pl.program_id(1)
        value = jnp.dot(token_ref[...], block[0], preferred_element_type=f32)
        span = pl.ds(pl.multiple_of(c * n, n), n)
        send_ref[k, span] = value[3 * n :].astype(bf16)
        for slot in range(3):
            keep_ref[slot, k, span] = value[slot * n : (slot + 1) * n]

    spec = pl.BlockSpec((1, depth, width), lambda k, c: (k, 0, c))
    pltpu.emit_pipeline(work, grid=(2, count), in_specs=[spec])(weight_ref.at[:, :, pl.ds(c0 * width, count * width)])


def partial_pre(chain, tokens, weight, c0, c1, width, vmem):
    rows, depth = tokens.shape
    n = rows // 4
    count = c1 - c0
    return chain.call(
        functools.partial(pre_kernel, c0, count, width),
        [in_vmem, in_hbm],
        [tokens, weight],
        [in_vmem, in_vmem],
        [jax.ShapeDtypeStruct((2, count * n, width), bf16), jax.ShapeDtypeStruct((3, 2, count * n, width), f32)],
        "partial_pre",
        vmem,
        4 * rows * depth * count * width,
        4 * depth * count * width,
    )


def hidden_kernel(width, spans, grad_ref, down_ref, *outs):
    depth = grad_ref.shape[1]

    def work(block):
        c = pl.program_id(0)
        value = lax.dot_general(grad_ref[...], block[...], (((1,), (1,)), ((), ())), preferred_element_type=f32)
        for (r0, r1, c0, c1), out in zip(spans, outs):
            n = r1 - r0

            @pl.when((c >= c0) & (c < c1))
            def _():
                out[pl.ds(pl.multiple_of((c - c0) * n, n), n)] = value[r0:r1]

    spec = pl.BlockSpec((width, depth), lambda c: (c, 0))
    pltpu.emit_pipeline(work, grid=(down_ref.shape[0] // width,), in_specs=[spec])(down_ref)


def hidden_grad(chain, cot, down, width, spans):
    rows, depth = cot.shape
    return chain.call(
        functools.partial(hidden_kernel, width, spans),
        [in_vmem, in_hbm],
        [cot, down],
        [in_vmem] * len(spans),
        [jax.ShapeDtypeStruct(((r1 - r0) * (c1 - c0), width), f32) for r0, r1, c0, c1 in spans],
        "hidden_grad",
        46,
        2 * rows * depth * down.shape[0],
        2 * depth * down.shape[0],
    )


def step_kernel(has, offsets, *refs):
    refs = list(refs)
    take = lambda: refs.pop(0)
    counts = {0: 1, 1: 3, 2: 4, 3: 2}
    inputs = {s: [take() for _ in range(counts[s])] for s in has}
    out_x, out_y = take(), take()
    if 0 in has:
        (send,) = inputs[0]
        at, size, _ = offsets[0]
        out_x[pl.ds(at, size)] = send[0]
        out_y[pl.ds(at, size)] = send[1]
    if 1 in has:
        keep, got_x, got_y = inputs[1]
        at, size, start = offsets[1]
        span = pl.ds(start, size)
        out_x[pl.ds(at, size)] = keep[1, 0].astype(bf16)
        out_x[pl.ds(at + size, size)] = (keep[1, 1] + got_y[span].astype(f32)).astype(bf16)
        out_y[pl.ds(at, size)] = (keep[2, 0] + got_x[span].astype(f32)).astype(bf16)
        out_y[pl.ds(at + size, size)] = keep[2, 1].astype(bf16)
    if 2 in has:
        keep, hidden, got_x, got_y = inputs[2]
        at, size, start = offsets[2]
        own = take()
        gate = keep[0, 0] + got_x[pl.ds(start, size)].astype(f32) + got_y[pl.ds(start, size)].astype(f32)
        upper = (
            keep[0, 1] + got_x[pl.ds(start + size, size)].astype(f32) + got_y[pl.ds(start + size, size)].astype(f32)
        )
        grad = hidden[...]
        sigma = jax.nn.sigmoid(gate)
        first = (grad * upper * sigma * (1.0 + gate * (1.0 - sigma))).astype(bf16)
        second = (grad * gate * sigma).astype(bf16)
        own[0] = first
        own[1] = second
        for out in (out_x, out_y):
            out[pl.ds(at, size)] = first
            out[pl.ds(at + size, size)] = second
    if 3 in has:
        got_x, got_y = inputs[3]
        at, size, start = offsets[3]
        out_x[pl.ds(at, size)] = got_y[pl.ds(start, size)]
        out_y[pl.ds(at, size)] = got_x[pl.ds(start + size, size)]


def gather_kernel(offset_one, offset_two, size, n, own, x_one, y_one, x_two, y_two, out):
    width = own.shape[2]
    for c in range(size // n):
        columns = pl.ds(c * width, width)
        rows = c * n
        for k in range(2):
            at = offset_one + k * size + rows
            out[k, pl.ds(0, n), columns] = own[k, pl.ds(rows, n)]
            out[k, pl.ds(n, n), columns] = x_one[pl.ds(at, n)]
            out[k, pl.ds(2 * n, n), columns] = y_one[pl.ds(at, n)]
        out[0, pl.ds(3 * n, n), columns] = x_two[pl.ds(offset_two + rows, n)]
        out[1, pl.ds(3 * n, n), columns] = y_two[pl.ds(offset_two + rows, n)]


class Exchange:
    def __init__(self, chain, units, lag, own_rows, width):
        self.chain, self.units, self.lag, self.width, self.own_rows = chain, units, lag, width, own_rows
        self.sends, self.keeps, self.hidden = {}, {}, {}
        self.got, self.place, self.own = {}, {}, {}

    def rows_in(self, u):
        return 2 * self.own_rows * len(self.units[u][0])

    def size_of(self, u):
        return (self.units[u][2] - self.units[u][1]) * self.rows_in(u)

    def stages(self, m):
        return {s: m - s * self.lag for s in range(4) if (m - s * self.lag) in self.units}

    def step(self, m):
        stages, lag = self.stages(m), self.lag
        pieces = (1, 2, 2, 1)
        offsets, at, operands = {}, 0, []
        for s, u in stages.items():
            size = self.size_of(u)
            offsets[s] = (at, size, self.place[u, s - 1] if s else 0)
            self.place[u, s] = at
            at += pieces[s] * size
            if s == 0:
                operands += [self.sends[u]]
            elif s == 1:
                operands += [self.keeps[u], *self.got[m - lag]]
            elif s == 2:
                operands += [self.keeps[u], self.hidden[u], *self.got[m - lag]]
            else:
                operands += [*self.got[m - lag]]
        shapes = [jax.ShapeDtypeStruct((at, self.width), bf16)] * 2
        if 2 in stages:
            shapes.append(jax.ShapeDtypeStruct((2, self.size_of(stages[2]), self.width), bf16))
        outs = self.chain.call(
            functools.partial(step_kernel, tuple(stages), offsets),
            [in_vmem] * len(operands),
            operands,
            [in_vmem] * len(shapes),
            shapes,
            "exchange_step",
            4,
            8 * at * self.width,
            8 * at * self.width,
        )
        self.got[m] = (swap(outs[0], 1), swap(outs[1], 2))
        if 2 in stages:
            self.own[stages[2]] = outs[2]

    def gather(self, u):
        n, columns = self.rows_in(u), (self.units[u][2] - self.units[u][1]) * self.width
        (out,) = self.chain.call(
            functools.partial(gather_kernel, self.place[u, 2], self.place[u, 3], self.size_of(u), n),
            [in_vmem] * 5,
            [self.own[u], *self.got[u + 2 * self.lag], *self.got[u + 3 * self.lag]],
            [in_vmem],
            [jax.ShapeDtypeStruct((2, 4 * n, columns), bf16)],
            "pre_grad",
            4,
            0,
            16 * n * columns,
        )
        return out


def shards(tokens, cotangent, gate_up, down_weight, first_code, first_scale, second_code, second_scale):
    groups = lax.axis_size("dp")
    bits = groups.bit_length() - 1
    chips = lax.axis_size("tensor") // 2
    me = lax.axis_index("dp")
    own, depth = tokens.shape
    rows, units = gate_up.shape[1:]
    width = 256 if units % 256 == 0 else 128
    chunks = units // width
    total_tokens = own * groups * lax.axis_size("tensor")
    orders = [list(range(bits)), list(reversed(range(bits)))]
    every = tuple(range(chips))
    rest = every[1:]
    staged = groups == 4 and chips == 4

    blocks = split_columns(tokens, groups, me)
    slots = [swap(block, s) if s else block for s, block in enumerate(blocks)]
    block = jnp.stack(slots)

    def near(value, axis):
        return pack([(v, 0, v.shape[axis]) for v in (value, pair(value))], axis)

    def send_on(value):
        return [onward(value, k) for k in rest]

    def far(found, axis, *others):
        n = found[0].shape[axis]
        other = pair(pack([(v, 0, n) for v in found], axis, *others))
        pieces = []
        for at, v in enumerate(found):
            pieces += [(v, 0, n), (other, at * n, at * n + n)]
        return pack(pieces, axis)

    packed = {((0,), 0): near(block, 1)}
    sent = send_on(block)
    held = hold_until(cotangent, block)
    packed[(0,), 1] = near(held, 0)
    if not staged and rest:
        packed[rest, 0] = far(sent, 1)
        packed[rest, 1] = far(send_on(held), 0)

    if staged:
        last = chunks - max(1, (chunks * 3) // 7)
        plan = {0: ((0,), 0, last)}
        at = 4
        for c in range(0, last, 2):
            plan[at] = (rest, c, min(c + 2, last))
            at += 1
        plan[at] = (every[1:3], last, chunks)
        plan[at + 1] = ((every[3], 0), last, chunks)
    else:
        plan = {c: (every, c, c + 1) for c in range(chunks)}

    def rows_of(ks):
        for kind in range(2):
            if (ks, kind) not in packed and (rest, kind) in packed:
                pieces = []
                for k in ks:
                    n = 2 * own
                    pieces.append((packed[(0,), kind], 0, n) if k == 0 else (packed[rest, kind], (k - 1) * n, k * n))
                packed[ks, kind] = pack(pieces, 1 - kind)
        t = packed[ks, 0]
        return (t, packed.get((ks, 1)), t.reshape(-1, rows))

    expand = lambda scale: jnp.repeat(scale, 128, axis=2)

    def forward(ks, c0, c1):
        t, c, _ = rows_of(ks)
        n = t.shape[1]
        lo, hi = c0 * width, c1 * width
        pre = []
        for k in range(2):
            w = gate_up[k, :, lo:hi]
            dot = lambda pick: jnp.dot(
                jnp.concatenate([t[s] for s in pick], axis=0), w, preferred_element_type=f32
            ).reshape(len(pick), n, hi - lo)
            active = list(range(groups))
            got = {s: [] for s in active}
            for b in orders[k]:
                mask = 1 << b
                send = [s for s in active if s & mask]
                active = [s for s in active if not s & mask]
                out = dot(send)
                for at, s in enumerate(send):
                    for extra in got[s]:
                        out = out.at[at].add(extra.astype(f32)) if len(send) > 1 else out + extra.astype(f32)[None]
                back = swap(out.astype(bf16), mask)
                for at, s in enumerate(send):
                    got[s ^ mask].append(back[at])
            value = dot([0])[0]
            for extra in got[0]:
                value = value + extra.astype(f32)
            pre.append(value)
        gate, upper = pre
        hidden = lax.dot_general(
            c, down_weight[lo:hi], (((1,), (1,)), ((), ())), preferred_element_type=f32
        )
        sigma = jax.nn.sigmoid(gate)
        grads = (
            (hidden * upper * sigma * (1.0 + gate * (1.0 - sigma))).astype(bf16),
            (hidden * gate * sigma).astype(bf16),
        )
        full = []
        for k in range(2):
            held = {0: grads[k]}
            for b in reversed(orders[k]):
                mask = 1 << b
                keys = sorted(held)
                back = swap(jnp.stack([held[s] for s in keys]), mask)
                for at, s in enumerate(keys):
                    held[s ^ mask] = back[at]
            full.append(jnp.concatenate([held[s] for s in range(groups)], axis=0))
        return jnp.stack(full)

    product = lambda g, c0, c1: jnp.einsum(
        "ktf,kdf->td", g, gate_up[:, :, c0 * width : c1 * width], preferred_element_type=f32
    )
    sums = {}

    def add_input_grad(u, g):
        ks, c0, c1 = plan[u]
        term = product(g, c0, c1)
        sums[ks] = term if ks not in sums else sums[ks] + term
        return sums[ks]

    def split(ks):
        value = sums[ks].reshape(groups, len(ks), 2, own, rows)
        return {k: value[:, at] for at, k in enumerate(ks)}

    def across(partial, ks):
        theirs = pair(jnp.stack([partial[k][:, 1] for k in ks]).astype(bf16))
        mine = [partial[k][:, 0] + theirs[at].astype(f32) for at, k in enumerate(ks)]
        return [back(v.astype(bf16), k).astype(f32) if k else v for k, v in zip(ks, mine)]

    def partials():
        partial = {}
        for ks in sums:
            for k, part in split(ks).items():
                partial[k] = partial[k] + part if k in partial else part
        return partial

    grads = {}
    if staged:
        chain = Chain()
        lag = 2
        exchange = Exchange(chain, plan, lag, own, width)
        steps = [m for m in range(max(plan) + 3 * lag + 1) if exchange.stages(m)]
        result, tops = [None], {}

        def input_grad_start():
            partial = partials()
            halves = [every[1:3], (every[3], 0)]
            arrived = [across(partial, ks) for ks in halves]

            def wait():
                total = sum(arrived[1][::-1] + arrived[0], jnp.zeros((groups, own, rows), f32))
                moved.append(total.astype(bf16))
                chain.add(moved[0])

            return wait

        moved = []

        def start(u):
            exchange.sends[u], exchange.keeps[u] = partial_pre(
                chain, rows_of(plan[u][0])[2], gate_up, *plan[u][1:], width, 8 if u else 56
            )

        def hidden_first():
            return hidden_grad(chain, rows_of((0,))[1], down_weight, width, [(0, 2 * own, 0, last), (0, 2 * own, last, chunks)])

        def hidden_rest(first, tail):
            n = 2 * own
            cuts = [(0, 3 * n, c0, c1) for ks, c0, c1 in plan.values() if ks == rest]
            cuts += [(0, 2 * n, last, chunks), (2 * n, 3 * n, last, chunks)]
            found = hidden_grad(chain, rows_of(rest)[1], down_weight, width, cuts)
            exchange.hidden[0] = first
            units_of_rest = [u for u in plan if plan[u][0] == rest]
            for u, value in zip(units_of_rest, found):
                exchange.hidden[u] = value
            exchange.hidden[max(plan) - 1] = found[-2]
            both = jnp.stack([found[-1].reshape(chunks - last, n, width), tail.reshape(chunks - last, n, width)], axis=1)
            exchange.hidden[max(plan)] = both.reshape(-1, width)

        def finish(u):
            grads[u] = exchange.gather(u)

        def inputs(u):
            chain.add(add_input_grad(u, grads[u]))

        def update(c0, c1, vmem):
            parts = []
            for u, (ks, a, b) in plan.items():
                if a <= c0 and c1 <= b:
                    parts.append((rows_of(ks)[2], grads[u], (c0 - a) * width))
            *result[0], tops[c0, 0], tops[c0, 1] = weight_step(
                chain, vmem, parts, gate_up, first_code, first_wide, second_code, second_wide, result[0], c0 * width, (c1 - c0) * width, total_tokens
            )

        start(0)
        spans = [p[1:] for p in plan.values() if p[0] == rest]
        pending = []
        for place, m in enumerate(steps):
            exchange.step(m)
            if m == 0:
                exchange.hidden[0], hidden_tail = hidden_first()
            if m == lag:
                packed[rest, 0] = far(sent, 1, chain.tokens[0])
                cot_sent = send_on(hold_until(cotangent, packed[rest, 0]))
            if place + 1 < len(steps) and steps[place + 1] in plan:
                start(steps[place + 1])
            if m == 3 * lag:
                packed[rest, 1] = far(cot_sent, 0, chain.tokens[0])
                hidden_rest(exchange.hidden[0], hidden_tail)
            if m == 4 * lag:
                first_wide = expand(hold_until(first_scale, chain.tokens[0]))
                second_wide = expand(hold_until(second_scale, chain.tokens[0]))
                chain.add(first_wide)
                chain.add(second_wide)
            done = m - 4 * lag
            if done in plan:
                finish(done)
                inputs(done)
                if plan[done][0] == rest:
                    pending.append(plan[done][1:])
            if pending and place + 1 < len(steps):
                update(*pending.pop(0), 20)
        for u in plan:
            if u not in grads:
                finish(u)
                inputs(u)
        wait = input_grad_start()
        for span in pending:
            update(*span, 20)
        wait()
        update(last, chunks, 44)
        outs = result[0]
        moved = moved[0]
    else:
        for u, unit in plan.items():
            grads[u] = forward(*unit)
            add_input_grad(u, grads[u])
        moved = sum(across(partials(), every), jnp.zeros((groups, own, rows), f32)).astype(bf16)

    final = jnp.stack([moved[0]] + [swap(moved[s], s) for s in range(1, groups)])
    final = jnp.stack([lax.dynamic_index_in_dim(final, me ^ a, 0, keepdims=False) for a in range(groups)], axis=1)
    input_grad = final.reshape(own, depth)

    if not staged:
        first_wide, second_wide = expand(first_scale), expand(second_scale)
        chain, outs, tops = Chain(), None, {}
        for c, (ks, c0, c1) in plan.items():
            *outs, tops[c0, 0], tops[c0, 1] = weight_step(
                chain,
                20,
                [(rows_of(ks)[2], grads[c], 0)],
                gate_up,
                first_code,
                first_wide,
                second_code,
                second_wide,
                outs,
                c0 * width,
                (c1 - c0) * width,
                total_tokens,
            )
    updated, code_one, code_two = outs
    scales = [jnp.concatenate([tops[c, i] for c, j in sorted(tops) if i == j], axis=0) for i in range(2)]
    scales = [jnp.transpose(scale, (1, 2, 0)) for scale in scales]
    return (input_grad, updated, code_one, scales[0], code_two, scales[1])


def solution(mesh):
    placed = (
        P(("dp", "tensor"), None),
        P(("dp", "tensor"), None),
        P(None, "dp", "tensor"),
        P("tensor", None),
        P(None, "dp", "tensor"),
        P(None, "dp", "tensor"),
        P(None, "dp", "tensor"),
        P(None, "dp", "tensor"),
    )
    return jax.shard_map(
        shards,
        mesh=mesh,
        in_specs=placed,
        out_specs=(
            P(("dp", "tensor"), None),
            P(None, "dp", "tensor"),
            P(None, "dp", "tensor"),
            P(None, "dp", "tensor"),
            P(None, "dp", "tensor"),
            P(None, "dp", "tensor"),
        ),
        check_vma=False,
    )
```

```python
import functools

import jax
import jax.numpy as jnp
from jax import lax
from jax.experimental import pallas as pl
from jax.experimental.pallas import tpu as pltpu
from jax.sharding import PartitionSpec as P

learning_rate = 0.003
beta_first = 0.9
beta_second = 0.95
f32 = jnp.float32
bf16 = jnp.bfloat16
in_vmem = pl.BlockSpec(memory_space=pltpu.VMEM)
in_hbm = pl.BlockSpec(memory_space=pltpu.HBM)


def swap(value, mask):
    return lax.ppermute(value, "dp", [(p, p ^ mask) for p in range(lax.axis_size("dp"))])


def back(value, distance):
    size = lax.axis_size("tensor")
    return lax.ppermute(value, "tensor", [(p, (p - 2 * distance) % size) for p in range(size)])


def onward(value, distance):
    return back(value, -distance)


def ring(value):
    return onward(value, 1)


def pair(value):
    return lax.ppermute(value, "tensor", [(p, p ^ 1) for p in range(lax.axis_size("tensor"))])


def split_kernel(groups, rows, me_ref, tokens_ref, *outs):
    for s in range(groups):
        at = pl.multiple_of((me_ref[0] ^ s) * rows, 128)
        outs[s][...] = tokens_ref[:, pl.ds(at, rows)]


def split_columns(tokens, groups, me):
    own, depth = tokens.shape
    rows = depth // groups
    return pl.pallas_call(
        functools.partial(split_kernel, groups, rows),
        in_specs=[pl.BlockSpec(memory_space=pltpu.SMEM), in_vmem],
        out_specs=[in_vmem] * groups,
        out_shape=[jax.ShapeDtypeStruct((own, rows), bf16)] * groups,
        compiler_params=pltpu.CompilerParams(vmem_limit_bytes=4 << 20),
        name="split_columns",
    )(jnp.reshape(me, (1,)).astype(jnp.int32), tokens)


def hold_kernel(value_ref, *refs):
    refs[-1][...] = value_ref[...]


def hold_until(value, *others):
    return pl.pallas_call(
        hold_kernel,
        in_specs=[in_vmem] + [pl.BlockSpec(memory_space=pl.ANY)] * len(others),
        out_specs=in_vmem,
        out_shape=jax.ShapeDtypeStruct(value.shape, value.dtype),
        compiler_params=pltpu.CompilerParams(vmem_limit_bytes=4 << 20),
        name="hold",
    )(value, *others)


def pack_kernel(cuts, axis, *refs):
    out, at = refs[-1], 0
    for ref, (lo, hi) in zip(refs, cuts):
        if axis == 2:
            out[:, :, at : at + hi - lo] = ref[:, :, lo:hi]
        elif axis == 1:
            out[:, at : at + hi - lo] = ref[:, lo:hi]
        else:
            out[at : at + hi - lo] = ref[lo:hi]
        at += hi - lo


def pack(pieces, axis, *others):
    shape = list(pieces[0][0].shape)
    shape[axis] = sum(hi - lo for _, lo, hi in pieces)
    return pl.pallas_call(
        functools.partial(pack_kernel, [p[1:] for p in pieces], axis),
        in_specs=[in_vmem] * len(pieces) + [pl.BlockSpec(memory_space=pl.ANY)] * len(others),
        out_specs=in_vmem,
        out_shape=jax.ShapeDtypeStruct(tuple(shape), pieces[0][0].dtype),
        compiler_params=pltpu.CompilerParams(vmem_limit_bytes=12 << 20),
        cost_estimate=pl.CostEstimate(flops=1, bytes_accessed=1, transcendentals=0),
        name="pack",
    )(*[p[0] for p in pieces], *others)


class Chain:
    def __init__(self):
        self.tokens = []

    def add(self, value):
        self.tokens.append(value)

    def call(self, kernel, in_specs, operands, out_specs, out_shape, name, vmem, flops, read, scratch=(), aliases=None):
        inputs, held, outputs = len(operands), len(self.tokens), len(out_shape)

        def body(*refs):
            kernel(*refs[:inputs], *refs[inputs + held : inputs + held + outputs], *refs[inputs + held + outputs + 1 :])

        anywhere = pl.BlockSpec(memory_space=pl.ANY)
        outs = pl.pallas_call(
            body,
            in_specs=list(in_specs) + [anywhere] * held,
            out_specs=list(out_specs) + [anywhere],
            out_shape=list(out_shape) + [jax.ShapeDtypeStruct((8, 128), f32)],
            input_output_aliases=aliases or {},
            scratch_shapes=list(scratch),
            compiler_params=pltpu.CompilerParams(vmem_limit_bytes=vmem << 20),
            cost_estimate=pl.CostEstimate(flops=1, bytes_accessed=1, transcendentals=0),
            name=name,
        )(*operands, *self.tokens)
        self.tokens = [outs[-1]]
        return outs[:-1]


def weight_kernel(parts, total_tokens, starts, c0, columns, tile, *refs):
    token_refs = refs[:parts]
    grad_refs = refs[parts : 2 * parts]
    weight_hbm, first_hbm, first_scale, second_hbm, second_scale = refs[2 * parts : 2 * parts + 5]
    outs_hbm = refs[-13:-10]
    first_tops, second_tops, wide_scale, top_table, total, rows_max, held_in, held_out, sem_in, sem_out = refs[-10:]
    first_gain = (1.0 - beta_first) / float(total_tokens) ** 0.5
    second_gain = (1.0 - beta_second) / float(total_tokens)
    group = 8
    tiles = weight_hbm.shape[1] // tile
    ins_hbm = (weight_hbm, first_hbm, second_hbm)

    def place(i):
        return i // tiles, pl.ds(pl.multiple_of(i % tiles * tile, tile), tile)

    def copies(i, out):
        k, span = place(i)
        hbm, held, sem = (outs_hbm, held_out, sem_out) if out else (ins_hbm, held_in, sem_in)
        result = []
        for a in range(3):
            far = hbm[a].at[k, span, pl.ds(c0, columns)]
            near = held.at[a, k, span]
            result.append(pltpu.make_async_copy(*((near, far) if out else (far, near)), sem.at[a, i]))
        return result

    def begin(i, carry):
        for copy in copies(i, False):
            copy.start()
        return carry

    lax.fori_loop(0, 2 * tiles, begin, 0)
    for k in range(2):
        for lane in range(0, columns, 128):
            at_scale = pl.ds((c0 + lane) // 128, 1)
            shape = (first_scale.shape[1], 128)
            wide_scale[k, :, pl.ds(lane, 128)] = jnp.broadcast_to(first_scale[k, :, at_scale] * beta_first, shape)
            wide_scale[2 + k, :, pl.ds(lane, 128)] = jnp.broadcast_to(second_scale[k, :, at_scale] * beta_second, shape)

    def work(i, carry):
        k, span_all = place(i)
        value = None
        for token_ref, grad_ref, start in zip(token_refs, grad_refs, starts):
            term = lax.dot_general(
                token_ref[:, span_all],
                grad_ref[k, :, pl.ds(start, columns)],
                (((0,), (0,)), ((), ())),
                preferred_element_type=f32,
            )
            value = term if value is None else value + term
        total[...] = value
        for copy in copies(i, False):
            copy.wait()

        def body(at, carry):
            base = pl.multiple_of(at * group, group)
            blocks = pl.ds(pl.multiple_of(i % tiles * (tile // 16) + base, group), group)
            tops_one, tops_two = [], []
            for lane in range(0, columns, 128):
                side = pl.ds(lane, 128)
                slot = 2 * (lane // 128)
                scale_one = wide_scale[k, blocks, side]
                scale_two = wide_scale[2 + k, blocks, side]
                states = []
                for b in range(group):
                    near = pl.ds(pl.multiple_of(at * group * 16, group * 16) + b * 16, 16)
                    span = pl.ds(pl.multiple_of(i % tiles * tile + at * group * 16, group * 16) + b * 16, 16)
                    grad = total[near, side]
                    first = held_in[1, k, span, side].astype(f32) * scale_one[b : b + 1] + first_gain * grad
                    second = held_in[2, k, span, side].astype(f32) * scale_two[b : b + 1]
                    second = second + second_gain * (grad * grad)
                    root = second * lax.rsqrt(second)
                    step = (learning_rate * first) * pl.reciprocal(root + 1e-08, approx=True)
                    held_out[0, k, span, side] = (held_in[0, k, span, side].astype(f32) - step).astype(bf16)
                    size = jnp.abs(first)
                    rows_max[slot, pl.ds(b * 8, 8)] = jnp.maximum(size[:8], size[8:])
                    rows_max[slot + 1, pl.ds(b * 8, 8)] = jnp.maximum(second[:8], second[8:])
                    states.append((first, second))
                inverses = []
                for kind, tops in ((0, tops_one), (1, tops_two)):
                    peak = rows_max[slot + kind, pl.ds(0, group, stride=8)]
                    for j in range(1, 8):
                        peak = jnp.maximum(peak, rows_max[slot + kind, pl.ds(j, group, stride=8)])
                    top = jnp.max(peak, axis=1, keepdims=True) + 1e-06
                    tops.append(top)
                    wide = jnp.broadcast_to(top, (group, 128))
                    inverse = pl.reciprocal(wide, approx=True)
                    inverses.append(inverse * (2.0 - wide * inverse))
                for b, (first, second) in enumerate(states):
                    span = pl.ds(pl.multiple_of(i % tiles * tile + at * group * 16, group * 16) + b * 16, 16)
                    held_out[1, k, span, side] = (first * inverses[0][b : b + 1]).astype(bf16)
                    held_out[2, k, span, side] = (second * inverses[1][b : b + 1]).astype(bf16)
            top_table[k, blocks, pl.ds(0, columns // 128)] = jnp.concatenate(tops_one, axis=1)
            top_table[2 + k, blocks, pl.ds(0, columns // 128)] = jnp.concatenate(tops_two, axis=1)
            return carry

        lax.fori_loop(0, tile // (group * 16), body, 0)
        for copy in copies(i, True):
            copy.start()
        return carry

    lax.fori_loop(0, 2 * tiles, work, 0)

    def end(i, carry):
        for copy in copies(i, True):
            copy.wait()
        return carry

    for k in range(2):
        first_tops[:, k] = jnp.transpose(top_table[k])[: columns // 128]
        second_tops[:, k] = jnp.transpose(top_table[2 + k])[: columns // 128]
    lax.fori_loop(0, 2 * tiles, end, 0)


def weight_step(chain, vmem, parts, weight, first, first_scale, second, second_scale, outs, c0, columns, total_tokens):
    rows = weight.shape[1]
    tile = min(512, rows)
    n = len(parts)
    operands = [t for t, _, _ in parts] + [g for _, g, _ in parts] + [weight, first, first_scale, second, second_scale]
    specs = [in_vmem] * (2 * n) + [in_hbm, in_hbm, in_vmem, in_hbm, in_vmem]
    aliases = {}
    if outs is not None:
        aliases = {len(operands) + i: i for i in range(3)}
        specs += [in_hbm] * 3
        operands += list(outs)
    elements = 2 * rows * columns
    kernel = functools.partial(weight_kernel, n, total_tokens, [at for _, _, at in parts], c0, columns, tile)
    return chain.call(
        kernel,
        specs,
        operands,
        [in_hbm] * 3 + [in_vmem] * 2,
        [jax.ShapeDtypeStruct(weight.shape, bf16)] * 3
        + [jax.ShapeDtypeStruct((columns // 128, 2, rows // 16), f32)] * 2,
        "weight_step",
        vmem,
        2 * elements * sum(t.shape[0] for t, _, _ in parts) + 40 * elements,
        12 * elements,
        scratch=[
            pltpu.VMEM((4, rows // 16, columns), f32),
            pltpu.VMEM((4, rows // 16, 128), f32),
            pltpu.VMEM((tile, columns), f32),
            pltpu.VMEM((columns // 64, 64, 128), f32),
            pltpu.VMEM((3, 2, rows, columns), bf16),
            pltpu.VMEM((3, 2, rows, columns), bf16),
            pltpu.SemaphoreType.DMA((3, 2 * rows // tile)),
            pltpu.SemaphoreType.DMA((3, 2 * rows // tile)),
        ],
        aliases=aliases,
    )


def pre_kernel(c0, count, width, token_ref, weight_ref, send_ref, keep_ref, held, sem):
    n = token_ref.shape[0] // 4

    def copy(i):
        k, c = i // count, i % count
        columns = pl.ds(pl.multiple_of((c0 + c) * width, width), width)
        return pltpu.make_async_copy(weight_ref.at[k, :, columns], held.at[i], sem.at[i])

    def begin(i, carry):
        copy(i).start()
        return carry

    lax.fori_loop(0, 2 * count, begin, 0)

    def work(i, carry):
        k, c = i // count, i % count
        copy(i).wait()
        value = jnp.dot(token_ref[...], held[i], preferred_element_type=f32)
        span = pl.ds(pl.multiple_of(c * n, n), n)
        send_ref[k, span] = value[3 * n :].astype(bf16)
        for slot in range(3):
            keep_ref[slot, k, span] = value[slot * n : (slot + 1) * n]
        return carry

    lax.fori_loop(0, 2 * count, work, 0)


def partial_pre(chain, tokens, weight, c0, c1, width, vmem):
    rows, depth = tokens.shape
    n = rows // 4
    count = c1 - c0
    return chain.call(
        functools.partial(pre_kernel, c0, count, width),
        [in_vmem, in_hbm],
        [tokens, weight],
        [in_vmem, in_vmem],
        [jax.ShapeDtypeStruct((2, count * n, width), bf16), jax.ShapeDtypeStruct((3, 2, count * n, width), f32)],
        "partial_pre",
        vmem,
        4 * rows * depth * count * width,
        4 * depth * count * width,
        scratch=[pltpu.VMEM((2 * count, depth, width), bf16), pltpu.SemaphoreType.DMA((2 * count,))],
    )


def hidden_kernel(width, spans, grad_ref, down_ref, *refs):
    outs, held, sem = refs[: len(spans)], refs[-2], refs[-1]
    count = down_ref.shape[0] // width

    def copy(i):
        return pltpu.make_async_copy(down_ref.at[pl.ds(pl.multiple_of(i * width, width), width)], held.at[i], sem.at[i])

    def begin(i, carry):
        copy(i).start()
        return carry

    lax.fori_loop(0, count, begin, 0)

    def work(c, carry):
        copy(c).wait()
        value = jnp.transpose(
            lax.dot_general(held[c], grad_ref[...], (((1,), (1,)), ((), ())), preferred_element_type=f32)
        )
        for (r0, r1, c0, c1), out in zip(spans, outs):
            n = r1 - r0

            @pl.when((c >= c0) & (c < c1))
            def _():
                out[pl.ds(pl.multiple_of((c - c0) * n, n), n)] = value[r0:r1]

        return carry

    lax.fori_loop(0, count, work, 0)


def hidden_grad(chain, cot, down, width, spans, vmem):
    rows, depth = cot.shape
    return chain.call(
        functools.partial(hidden_kernel, width, spans),
        [in_vmem, in_hbm],
        [cot, down],
        [in_vmem] * len(spans),
        [jax.ShapeDtypeStruct(((r1 - r0) * (c1 - c0), width), f32) for r0, r1, c0, c1 in spans],
        "hidden_grad",
        vmem,
        2 * rows * depth * down.shape[0],
        2 * depth * down.shape[0],
        scratch=[
            pltpu.VMEM((down.shape[0] // width, width, depth), bf16),
            pltpu.SemaphoreType.DMA((down.shape[0] // width,)),
        ],
    )


def step_kernel(has, offsets, *refs):
    refs = list(refs)
    take = lambda: refs.pop(0)
    counts = {0: 1, 1: 3, 2: 4, 3: 2}
    inputs = {s: [take() for _ in range(counts[s])] for s in has}
    out_x, out_y = take(), take()
    if 0 in has:
        (send,) = inputs[0]
        at, size, _ = offsets[0]
        out_x[pl.ds(at, size)] = send[0]
        out_y[pl.ds(at, size)] = send[1]
    if 1 in has:
        keep, got_x, got_y = inputs[1]
        at, size, start = offsets[1]
        span = pl.ds(start, size)
        out_x[pl.ds(at, size)] = keep[1, 0].astype(bf16)
        out_x[pl.ds(at + size, size)] = (keep[1, 1] + got_y[span].astype(f32)).astype(bf16)
        out_y[pl.ds(at, size)] = (keep[2, 0] + got_x[span].astype(f32)).astype(bf16)
        out_y[pl.ds(at + size, size)] = keep[2, 1].astype(bf16)
    if 2 in has:
        keep, hidden, got_x, got_y = inputs[2]
        at, size, start = offsets[2]
        own = take()
        gate = keep[0, 0] + got_x[pl.ds(start, size)].astype(f32) + got_y[pl.ds(start, size)].astype(f32)
        upper = (
            keep[0, 1] + got_x[pl.ds(start + size, size)].astype(f32) + got_y[pl.ds(start + size, size)].astype(f32)
        )
        grad = hidden[...]
        sigma = jax.nn.sigmoid(gate)
        first = (grad * upper * sigma * (1.0 + gate * (1.0 - sigma))).astype(bf16)
        second = (grad * gate * sigma).astype(bf16)
        own[0] = first
        own[1] = second
        for out in (out_x, out_y):
            out[pl.ds(at, size)] = first
            out[pl.ds(at + size, size)] = second
    if 3 in has:
        got_x, got_y = inputs[3]
        at, size, start = offsets[3]
        out_x[pl.ds(at, size)] = got_y[pl.ds(start, size)]
        out_y[pl.ds(at, size)] = got_x[pl.ds(start + size, size)]


def gather_kernel(offset_one, offset_two, size, n, own, x_one, y_one, x_two, y_two, out):
    width = own.shape[2]
    for c in range(size // n):
        columns = pl.ds(c * width, width)
        rows = c * n
        for k in range(2):
            at = offset_one + k * size + rows
            out[k, pl.ds(0, n), columns] = own[k, pl.ds(rows, n)]
            out[k, pl.ds(n, n), columns] = x_one[pl.ds(at, n)]
            out[k, pl.ds(2 * n, n), columns] = y_one[pl.ds(at, n)]
        out[0, pl.ds(3 * n, n), columns] = x_two[pl.ds(offset_two + rows, n)]
        out[1, pl.ds(3 * n, n), columns] = y_two[pl.ds(offset_two + rows, n)]


class Exchange:
    def __init__(self, chain, units, lag, own_rows, width):
        self.chain, self.units, self.lag, self.width, self.own_rows = chain, units, lag, width, own_rows
        self.sends, self.keeps, self.hidden = {}, {}, {}
        self.got, self.place, self.own = {}, {}, {}

    def rows_in(self, u):
        return 2 * self.own_rows * len(self.units[u][0])

    def size_of(self, u):
        return (self.units[u][2] - self.units[u][1]) * self.rows_in(u)

    def stages(self, m):
        return {s: m - s * self.lag for s in range(4) if (m - s * self.lag) in self.units}

    def step(self, m):
        stages, lag = self.stages(m), self.lag
        pieces = (1, 2, 2, 1)
        offsets, at, operands = {}, 0, []
        for s, u in stages.items():
            size = self.size_of(u)
            offsets[s] = (at, size, self.place[u, s - 1] if s else 0)
            self.place[u, s] = at
            at += pieces[s] * size
            if s == 0:
                operands += [self.sends[u]]
            elif s == 1:
                operands += [self.keeps[u], *self.got[m - lag]]
            elif s == 2:
                operands += [self.keeps[u], self.hidden[u], *self.got[m - lag]]
            else:
                operands += [*self.got[m - lag]]
        shapes = [jax.ShapeDtypeStruct((at, self.width), bf16)] * 2
        if 2 in stages:
            shapes.append(jax.ShapeDtypeStruct((2, self.size_of(stages[2]), self.width), bf16))
        outs = self.chain.call(
            functools.partial(step_kernel, tuple(stages), offsets),
            [in_vmem] * len(operands),
            operands,
            [in_vmem] * len(shapes),
            shapes,
            "exchange_step",
            12,
            8 * at * self.width,
            8 * at * self.width,
        )
        self.got[m] = (swap(outs[0], 1), swap(outs[1], 2))
        if 2 in stages:
            self.own[stages[2]] = outs[2]

    def gather(self, u):
        n, columns = self.rows_in(u), (self.units[u][2] - self.units[u][1]) * self.width
        (out,) = self.chain.call(
            functools.partial(gather_kernel, self.place[u, 2], self.place[u, 3], self.size_of(u), n),
            [in_vmem] * 5,
            [self.own[u], *self.got[u + 2 * self.lag], *self.got[u + 3 * self.lag]],
            [in_vmem],
            [jax.ShapeDtypeStruct((2, 4 * n, columns), bf16)],
            "pre_grad",
            8,
            0,
            16 * n * columns,
        )
        return out


def shards(tokens, cotangent, gate_up, down_weight, first_code, first_scale, second_code, second_scale):
    groups = lax.axis_size("dp")
    bits = groups.bit_length() - 1
    chips = lax.axis_size("tensor") // 2
    me = lax.axis_index("dp")
    own, depth = tokens.shape
    rows, units = gate_up.shape[1:]
    width = 256 if units % 256 == 0 else 128
    chunks = units // width
    total_tokens = own * groups * lax.axis_size("tensor")
    orders = [list(range(bits)), list(reversed(range(bits)))]
    every = tuple(range(chips))
    rest = every[1:]
    staged = groups == 4 and chips == 4

    blocks = split_columns(tokens, groups, me)
    slots = [swap(block, s) if s else block for s, block in enumerate(blocks)]
    block = jnp.stack(slots)

    def near(value, axis, *others):
        return pack([(v, 0, v.shape[axis]) for v in (value, pair(value))], axis, *others)

    def send_on(value):
        return [onward(value, k) for k in rest]

    def far(found, axis, *others):
        n = found[0].shape[axis]
        other = pair(pack([(v, 0, n) for v in found], axis, *others))
        pieces = []
        for at, v in enumerate(found):
            pieces += [(v, 0, n), (other, at * n, at * n + n)]
        return pack(pieces, axis)

    packed = {((0,), 0): near(block, 1)}
    sent = send_on(block)
    packed[(0,), 1] = near(cotangent, 0, block)
    if not staged and rest:
        packed[rest, 0] = far(sent, 1)
        packed[rest, 1] = far(send_on(cotangent), 0)

    if staged:
        last = chunks - max(1, (chunks * 3) // 7)
        second = 7
        plan = {0: ((0,), 0, last)}
        plan[4] = (rest, 0, last)
        plan[second] = (every, last, chunks)
    else:
        plan = {c: (every, c, c + 1) for c in range(chunks)}

    def rows_of(ks):
        for kind in range(2):
            if (ks, kind) not in packed and (rest, kind) in packed:
                pieces = []
                for k in ks:
                    n = 2 * own
                    pieces.append((packed[(0,), kind], 0, n) if k == 0 else (packed[rest, kind], (k - 1) * n, k * n))
                packed[ks, kind] = pack(pieces, 1 - kind)
        t = packed[ks, 0]
        return (t, packed.get((ks, 1)), t.reshape(-1, rows))


    def forward(ks, c0, c1):
        t, c, _ = rows_of(ks)
        n = t.shape[1]
        lo, hi = c0 * width, c1 * width
        pre = []
        for k in range(2):
            w = gate_up[k, :, lo:hi]
            dot = lambda pick: jnp.dot(
                jnp.concatenate([t[s] for s in pick], axis=0), w, preferred_element_type=f32
            ).reshape(len(pick), n, hi - lo)
            active = list(range(groups))
            got = {s: [] for s in active}
            for b in orders[k]:
                mask = 1 << b
                send = [s for s in active if s & mask]
                active = [s for s in active if not s & mask]
                out = dot(send)
                for at, s in enumerate(send):
                    for extra in got[s]:
                        out = out.at[at].add(extra.astype(f32)) if len(send) > 1 else out + extra.astype(f32)[None]
                back = swap(out.astype(bf16), mask)
                for at, s in enumerate(send):
                    got[s ^ mask].append(back[at])
            value = dot([0])[0]
            for extra in got[0]:
                value = value + extra.astype(f32)
            pre.append(value)
        gate, upper = pre
        hidden = lax.dot_general(
            c, down_weight[lo:hi], (((1,), (1,)), ((), ())), preferred_element_type=f32
        )
        sigma = jax.nn.sigmoid(gate)
        grads = (
            (hidden * upper * sigma * (1.0 + gate * (1.0 - sigma))).astype(bf16),
            (hidden * gate * sigma).astype(bf16),
        )
        full = []
        for k in range(2):
            held = {0: grads[k]}
            for b in reversed(orders[k]):
                mask = 1 << b
                keys = sorted(held)
                back = swap(jnp.stack([held[s] for s in keys]), mask)
                for at, s in enumerate(keys):
                    held[s ^ mask] = back[at]
            full.append(jnp.concatenate([held[s] for s in range(groups)], axis=0))
        return jnp.stack(full)

    product = lambda g, c0, c1: jnp.einsum(
        "ktf,kdf->td", g, gate_up[:, :, c0 * width : c1 * width], preferred_element_type=f32
    )
    sums = {}

    def add_input_grad(u, g):
        ks, c0, c1 = plan[u]
        term = product(g, c0, c1)
        sums[ks] = term if ks not in sums else sums[ks] + term
        return sums[ks]

    def split(ks):
        value = sums[ks].reshape(groups, len(ks), 2, own, rows)
        return {k: value[:, at] for at, k in enumerate(ks)}

    def across(partial, ks):
        theirs = pair(jnp.stack([partial[k][:, 1] for k in ks]).astype(bf16))
        mine = [partial[k][:, 0] + theirs[at].astype(f32) for at, k in enumerate(ks)]
        return [back(v.astype(bf16), k).astype(f32) if k else v for k, v in zip(ks, mine)]

    def partials():
        partial = {}
        for ks in sums:
            for k, part in split(ks).items():
                partial[k] = partial[k] + part if k in partial else part
        return partial

    grads = {}
    if staged:
        chain = Chain()
        lag = 2
        exchange = Exchange(chain, plan, lag, own, width)
        steps = [m for m in range(max(plan) + 3 * lag + 1) if exchange.stages(m)]
        result, tops = [None], {}

        def input_grad_start():
            arrived = across(partials(), every)

            def wait():
                moved.append(sum(arrived).astype(bf16))
                chain.add(moved[0])

            return wait

        moved = []

        def start(u):
            exchange.sends[u], exchange.keeps[u] = partial_pre(
                chain, rows_of(plan[u][0])[2], gate_up, *plan[u][1:], width, 12 if u else 56
            )

        def hidden_first():
            return hidden_grad(chain, rows_of((0,))[1], down_weight, width, [(0, 2 * own, 0, last), (0, 2 * own, last, chunks)], 56)

        def hidden_rest(first, tail):
            n = 2 * own
            cuts = [(0, 3 * n, 0, last), (0, 3 * n, last, chunks)]
            found = hidden_grad(chain, rows_of(rest)[1], down_weight, width, cuts, 24)
            exchange.hidden[4] = found[0]
            both = [tail.reshape(chunks - last, n, width), found[1].reshape(chunks - last, 3 * n, width)]
            exchange.hidden[second] = pack([(v, 0, v.shape[1]) for v in both], 1).reshape(-1, width)

        def finish(u):
            grads[u] = exchange.gather(u)

        def inputs(u):
            chain.add(add_input_grad(u, grads[u]))

        def update(c0, c1, vmem):
            parts = []
            for u, (ks, a, b) in plan.items():
                if a <= c0 and c1 <= b:
                    parts.append((rows_of(ks)[2], grads[u], (c0 - a) * width))
            *result[0], tops[c0, 0], tops[c0, 1] = weight_step(
                chain, vmem, parts, gate_up, first_code, first_scale, second_code, second_scale, result[0], c0 * width, (c1 - c0) * width, total_tokens
            )

        start(0)
        for place, m in enumerate(steps):
            exchange.step(m)
            token = chain.tokens[0]
            if m == lag:
                packed[rest, 0] = far(sent, 1, token)
                exchange.hidden[0], hidden_tail = hidden_first()
            elif m == 2 * lag:
                cot_sent = send_on(hold_until(cotangent, token))
            elif m == 4 * lag - 1:
                packed[rest, 1] = far(cot_sent, 0, token)
                hidden_rest(exchange.hidden[0], hidden_tail)
            if place + 1 < len(steps) and steps[place + 1] in plan:
                start(steps[place + 1])
            if m == 4 * lag:
                finish(0)
                inputs(0)
            if m == second + 2 * lag:
                finish(4)
                inputs(4)
                update(0, last // 2, 20)
        finish(second)
        inputs(second)
        wait = input_grad_start()
        update(last // 2, last, 44)
        update(last, chunks - 1, 44)
        wait()
        update(chunks - 1, chunks, 44)
        outs = result[0]
        moved = moved[0]
    else:
        for u, unit in plan.items():
            grads[u] = forward(*unit)
            add_input_grad(u, grads[u])
        moved = sum(across(partials(), every), jnp.zeros((groups, own, rows), f32)).astype(bf16)

    final = jnp.stack([moved[0]] + [swap(moved[s], s) for s in range(1, groups)])
    final = jnp.stack([lax.dynamic_index_in_dim(final, me ^ a, 0, keepdims=False) for a in range(groups)], axis=1)
    input_grad = final.reshape(own, depth)

    if not staged:
        chain, outs, tops = Chain(), None, {}
        for c, (ks, c0, c1) in plan.items():
            *outs, tops[c0, 0], tops[c0, 1] = weight_step(
                chain,
                20,
                [(rows_of(ks)[2], grads[c], 0)],
                gate_up,
                first_code,
                first_scale,
                second_code,
                second_scale,
                outs,
                c0 * width,
                (c1 - c0) * width,
                total_tokens,
            )
    updated, code_one, code_two = outs
    scales = [jnp.concatenate([tops[c, i] for c, j in sorted(tops) if i == j], axis=0) for i in range(2)]
    scales = [jnp.transpose(scale, (1, 2, 0)) for scale in scales]
    return (input_grad, updated, code_one, scales[0], code_two, scales[1])


def solution(mesh):
    placed = (
        P(("dp", "tensor"), None),
        P(("dp", "tensor"), None),
        P(None, "dp", "tensor"),
        P("tensor", None),
        P(None, "dp", "tensor"),
        P(None, "dp", "tensor"),
        P(None, "dp", "tensor"),
        P(None, "dp", "tensor"),
    )
    return jax.shard_map(
        shards,
        mesh=mesh,
        in_specs=placed,
        out_specs=(
            P(("dp", "tensor"), None),
            P(None, "dp", "tensor"),
            P(None, "dp", "tensor"),
            P(None, "dp", "tensor"),
            P(None, "dp", "tensor"),
            P(None, "dp", "tensor"),
        ),
        check_vma=False,
    )
```

```python
import functools

import jax
import jax.numpy as jnp
from jax import lax
from jax.experimental import pallas as pl
from jax.experimental.pallas import tpu as pltpu
from jax.sharding import PartitionSpec as P

learning_rate = 0.003
beta_first = 0.9
beta_second = 0.95
f32 = jnp.float32
bf16 = jnp.bfloat16
in_vmem = pl.BlockSpec(memory_space=pltpu.VMEM)
in_hbm = pl.BlockSpec(memory_space=pltpu.HBM)


def swap(value, mask):
    return lax.ppermute(value, "dp", [(p, p ^ mask) for p in range(lax.axis_size("dp"))])


def back(value, distance):
    size = lax.axis_size("tensor")
    return lax.ppermute(value, "tensor", [(p, (p - 2 * distance) % size) for p in range(size)])


def onward(value, distance):
    return back(value, -distance)


def ring(value):
    return onward(value, 1)


def pair(value):
    return lax.ppermute(value, "tensor", [(p, p ^ 1) for p in range(lax.axis_size("tensor"))])


def split_kernel(groups, rows, me_ref, tokens_ref, *outs):
    for s in range(groups):
        at = pl.multiple_of((me_ref[0] ^ s) * rows, 128)
        outs[s][...] = tokens_ref[:, pl.ds(at, rows)]


def split_columns(tokens, groups, me):
    own, depth = tokens.shape
    rows = depth // groups
    return pl.pallas_call(
        functools.partial(split_kernel, groups, rows),
        in_specs=[pl.BlockSpec(memory_space=pltpu.SMEM), in_vmem],
        out_specs=[in_vmem] * groups,
        out_shape=[jax.ShapeDtypeStruct((own, rows), bf16)] * groups,
        compiler_params=pltpu.CompilerParams(vmem_limit_bytes=4 << 20),
        name="split_columns",
    )(jnp.reshape(me, (1,)).astype(jnp.int32), tokens)


def hold_kernel(value_ref, *refs):
    refs[-1][...] = value_ref[...]


def hold_until(value, *others):
    return pl.pallas_call(
        hold_kernel,
        in_specs=[in_vmem] + [pl.BlockSpec(memory_space=pl.ANY)] * len(others),
        out_specs=in_vmem,
        out_shape=jax.ShapeDtypeStruct(value.shape, value.dtype),
        compiler_params=pltpu.CompilerParams(vmem_limit_bytes=4 << 20),
        name="hold",
    )(value, *others)


def pack_kernel(cuts, axis, *refs):
    out, at = refs[-1], 0
    for ref, (lo, hi) in zip(refs, cuts):
        if axis == 2:
            out[:, :, at : at + hi - lo] = ref[:, :, lo:hi]
        elif axis == 1:
            out[:, at : at + hi - lo] = ref[:, lo:hi]
        else:
            out[at : at + hi - lo] = ref[lo:hi]
        at += hi - lo


def pack(pieces, axis, *others):
    shape = list(pieces[0][0].shape)
    shape[axis] = sum(hi - lo for _, lo, hi in pieces)
    return pl.pallas_call(
        functools.partial(pack_kernel, [p[1:] for p in pieces], axis),
        in_specs=[in_vmem] * len(pieces) + [pl.BlockSpec(memory_space=pl.ANY)] * len(others),
        out_specs=in_vmem,
        out_shape=jax.ShapeDtypeStruct(tuple(shape), pieces[0][0].dtype),
        compiler_params=pltpu.CompilerParams(vmem_limit_bytes=12 << 20),
        cost_estimate=pl.CostEstimate(flops=1, bytes_accessed=1, transcendentals=0),
        name="pack",
    )(*[p[0] for p in pieces], *others)


class Chain:
    def __init__(self):
        self.tokens = []

    def add(self, value):
        self.tokens.append(value)

    def call(self, kernel, in_specs, operands, out_specs, out_shape, name, vmem, flops, read, scratch=(), aliases=None):
        inputs, held, outputs = len(operands), len(self.tokens), len(out_shape)

        def body(*refs):
            kernel(*refs[:inputs], *refs[inputs + held : inputs + held + outputs], *refs[inputs + held + outputs + 1 :])

        anywhere = pl.BlockSpec(memory_space=pl.ANY)
        outs = pl.pallas_call(
            body,
            in_specs=list(in_specs) + [anywhere] * held,
            out_specs=list(out_specs) + [anywhere],
            out_shape=list(out_shape) + [jax.ShapeDtypeStruct((8, 128), f32)],
            input_output_aliases=aliases or {},
            scratch_shapes=list(scratch),
            compiler_params=pltpu.CompilerParams(vmem_limit_bytes=vmem << 20),
            cost_estimate=pl.CostEstimate(flops=1, bytes_accessed=1, transcendentals=0),
            name=name,
        )(*operands, *self.tokens)
        self.tokens = [outs[-1]]
        return outs[:-1]


def weight_kernel(parts, total_tokens, starts, c0, columns, tile, *refs):
    token_refs = refs[:parts]
    grad_refs = refs[parts : 2 * parts]
    weight_hbm, first_hbm, first_scale, second_hbm, second_scale = refs[2 * parts : 2 * parts + 5]
    outs_hbm = refs[-13:-10]
    first_tops, second_tops, wide_scale, top_table, total, rows_max, held_in, held_out, sem_in, sem_out = refs[-10:]
    first_gain = (1.0 - beta_first) / float(total_tokens) ** 0.5
    second_gain = (1.0 - beta_second) / float(total_tokens)
    group = 8
    tiles = weight_hbm.shape[1] // tile
    ins_hbm = (weight_hbm, first_hbm, second_hbm)

    def place(i):
        return i // tiles, pl.ds(pl.multiple_of(i % tiles * tile, tile), tile)

    def copies(i, out):
        k, span = place(i)
        hbm, held, sem = (outs_hbm, held_out, sem_out) if out else (ins_hbm, held_in, sem_in)
        result = []
        for a in range(3):
            far = hbm[a].at[k, span, pl.ds(c0, columns)]
            near = held.at[a, k, span]
            result.append(pltpu.make_async_copy(*((near, far) if out else (far, near)), sem.at[a, i]))
        return result

    def begin(i, carry):
        for copy in copies(i, False):
            copy.start()
        return carry

    lax.fori_loop(0, 2 * tiles, begin, 0)
    for k in range(2):
        for lane in range(0, columns, 128):
            at_scale = pl.ds((c0 + lane) // 128, 1)
            shape = (first_scale.shape[1], 128)
            wide_scale[k, :, pl.ds(lane, 128)] = jnp.broadcast_to(first_scale[k, :, at_scale] * beta_first, shape)
            wide_scale[2 + k, :, pl.ds(lane, 128)] = jnp.broadcast_to(second_scale[k, :, at_scale] * beta_second, shape)

    def work(i, carry):
        k, span_all = place(i)
        value = None
        for token_ref, grad_ref, start in zip(token_refs, grad_refs, starts):
            term = lax.dot_general(
                token_ref[:, span_all],
                grad_ref[k, :, pl.ds(start, columns)],
                (((0,), (0,)), ((), ())),
                preferred_element_type=f32,
            )
            value = term if value is None else value + term
        total[...] = value
        for copy in copies(i, False):
            copy.wait()

        def body(at, carry):
            base = pl.multiple_of(at * group, group)
            blocks = pl.ds(pl.multiple_of(i % tiles * (tile // 16) + base, group), group)
            tops_one, tops_two = [], []
            for lane in range(0, columns, 128):
                side = pl.ds(lane, 128)
                slot = 2 * (lane // 128)
                scale_one = wide_scale[k, blocks, side]
                scale_two = wide_scale[2 + k, blocks, side]
                states = []
                for b in range(group):
                    near = pl.ds(pl.multiple_of(at * group * 16, group * 16) + b * 16, 16)
                    span = pl.ds(pl.multiple_of(i % tiles * tile + at * group * 16, group * 16) + b * 16, 16)
                    grad = total[near, side]
                    first = held_in[1, k, span, side].astype(f32) * scale_one[b : b + 1] + first_gain * grad
                    second = held_in[2, k, span, side].astype(f32) * scale_two[b : b + 1]
                    second = second + second_gain * (grad * grad)
                    root = second * lax.rsqrt(second)
                    step = (learning_rate * first) * pl.reciprocal(root + 1e-08, approx=True)
                    held_out[0, k, span, side] = (held_in[0, k, span, side].astype(f32) - step).astype(bf16)
                    size = jnp.abs(first)
                    rows_max[slot, pl.ds(b * 8, 8)] = jnp.maximum(size[:8], size[8:])
                    rows_max[slot + 1, pl.ds(b * 8, 8)] = jnp.maximum(second[:8], second[8:])
                    states.append((first, second))
                inverses = []
                for kind, tops in ((0, tops_one), (1, tops_two)):
                    peak = rows_max[slot + kind, pl.ds(0, group, stride=8)]
                    for j in range(1, 8):
                        peak = jnp.maximum(peak, rows_max[slot + kind, pl.ds(j, group, stride=8)])
                    top = jnp.max(peak, axis=1, keepdims=True) + 1e-06
                    tops.append(top)
                    wide = jnp.broadcast_to(top, (group, 128))
                    inverse = pl.reciprocal(wide, approx=True)
                    inverses.append(inverse * (2.0 - wide * inverse))
                for b, (first, second) in enumerate(states):
                    span = pl.ds(pl.multiple_of(i % tiles * tile + at * group * 16, group * 16) + b * 16, 16)
                    held_out[1, k, span, side] = (first * inverses[0][b : b + 1]).astype(bf16)
                    held_out[2, k, span, side] = (second * inverses[1][b : b + 1]).astype(bf16)
            top_table[k, blocks, pl.ds(0, columns // 128)] = jnp.concatenate(tops_one, axis=1)
            top_table[2 + k, blocks, pl.ds(0, columns // 128)] = jnp.concatenate(tops_two, axis=1)
            return carry

        lax.fori_loop(0, tile // (group * 16), body, 0)
        for copy in copies(i, True):
            copy.start()
        return carry

    lax.fori_loop(0, 2 * tiles, work, 0)

    def end(i, carry):
        for copy in copies(i, True):
            copy.wait()
        return carry

    for k in range(2):
        first_tops[:, k] = jnp.transpose(top_table[k])[: columns // 128]
        second_tops[:, k] = jnp.transpose(top_table[2 + k])[: columns // 128]
    lax.fori_loop(0, 2 * tiles, end, 0)


def weight_step(chain, vmem, parts, weight, first, first_scale, second, second_scale, outs, c0, columns, total_tokens):
    rows = weight.shape[1]
    tile = min(512, rows)
    n = len(parts)
    operands = [t for t, _, _ in parts] + [g for _, g, _ in parts] + [weight, first, first_scale, second, second_scale]
    specs = [in_vmem] * (2 * n) + [in_hbm, in_hbm, in_vmem, in_hbm, in_vmem]
    aliases = {}
    if outs is not None:
        aliases = {len(operands) + i: i for i in range(3)}
        specs += [in_hbm] * 3
        operands += list(outs)
    elements = 2 * rows * columns
    kernel = functools.partial(weight_kernel, n, total_tokens, [at for _, _, at in parts], c0, columns, tile)
    return chain.call(
        kernel,
        specs,
        operands,
        [in_hbm] * 3 + [in_vmem] * 2,
        [jax.ShapeDtypeStruct(weight.shape, bf16)] * 3
        + [jax.ShapeDtypeStruct((columns // 128, 2, rows // 16), f32)] * 2,
        "weight_step",
        vmem,
        2 * elements * sum(t.shape[0] for t, _, _ in parts) + 40 * elements,
        12 * elements,
        scratch=[
            pltpu.VMEM((4, rows // 16, columns), f32),
            pltpu.VMEM((4, rows // 16, 128), f32),
            pltpu.VMEM((tile, columns), f32),
            pltpu.VMEM((columns // 64, 72, 128), f32),
            pltpu.VMEM((3, 2, rows, columns), bf16),
            pltpu.VMEM((3, 2, rows, columns), bf16),
            pltpu.SemaphoreType.DMA((3, 2 * rows // tile)),
            pltpu.SemaphoreType.DMA((3, 2 * rows // tile)),
        ],
        aliases=aliases,
    )


def pre_kernel(c0, count, width, token_ref, weight_ref, send_ref, keep_ref, held, sem):
    n = token_ref.shape[0] // 4

    def copy(i):
        k, c = i // count, i % count
        columns = pl.ds(pl.multiple_of((c0 + c) * width, width), width)
        return pltpu.make_async_copy(weight_ref.at[k, :, columns], held.at[i], sem.at[i])

    def begin(i, carry):
        copy(i).start()
        return carry

    lax.fori_loop(0, 2 * count, begin, 0)

    def work(i, carry):
        k, c = i // count, i % count
        copy(i).wait()
        value = jnp.dot(token_ref[...], held[i], preferred_element_type=f32)
        span = pl.ds(pl.multiple_of(c * n, n), n)
        send_ref[k, span] = value[3 * n :].astype(bf16)
        for slot in range(3):
            keep_ref[slot, k, span] = value[slot * n : (slot + 1) * n]
        return carry

    lax.fori_loop(0, 2 * count, work, 0)


def partial_pre(chain, tokens, weight, c0, c1, width, vmem):
    rows, depth = tokens.shape
    n = rows // 4
    count = c1 - c0
    return chain.call(
        functools.partial(pre_kernel, c0, count, width),
        [in_vmem, in_hbm],
        [tokens, weight],
        [in_vmem, in_vmem],
        [jax.ShapeDtypeStruct((2, count * n, width), bf16), jax.ShapeDtypeStruct((3, 2, count * n, width), f32)],
        "partial_pre",
        vmem,
        4 * rows * depth * count * width,
        4 * depth * count * width,
        scratch=[pltpu.VMEM((2 * count, depth, width), bf16), pltpu.SemaphoreType.DMA((2 * count,))],
    )


def hidden_kernel(width, spans, grad_ref, down_ref, *refs):
    outs, held, sem = refs[: len(spans)], refs[-2], refs[-1]
    count = down_ref.shape[0] // width

    def copy(i):
        return pltpu.make_async_copy(down_ref.at[pl.ds(pl.multiple_of(i * width, width), width)], held.at[i], sem.at[i])

    def begin(i, carry):
        copy(i).start()
        return carry

    lax.fori_loop(0, count, begin, 0)

    def work(c, carry):
        copy(c).wait()
        value = jnp.transpose(
            lax.dot_general(held[c], grad_ref[...], (((1,), (1,)), ((), ())), preferred_element_type=f32)
        )
        for (r0, r1, c0, c1), out in zip(spans, outs):
            n = r1 - r0

            @pl.when((c >= c0) & (c < c1))
            def _():
                out[pl.ds(pl.multiple_of((c - c0) * n, n), n)] = value[r0:r1]

        return carry

    lax.fori_loop(0, count, work, 0)


def hidden_grad(chain, cot, down, width, spans, vmem):
    rows, depth = cot.shape
    return chain.call(
        functools.partial(hidden_kernel, width, spans),
        [in_vmem, in_hbm],
        [cot, down],
        [in_vmem] * len(spans),
        [jax.ShapeDtypeStruct(((r1 - r0) * (c1 - c0), width), f32) for r0, r1, c0, c1 in spans],
        "hidden_grad",
        vmem,
        2 * rows * depth * down.shape[0],
        2 * depth * down.shape[0],
        scratch=[
            pltpu.VMEM((down.shape[0] // width, width, depth), bf16),
            pltpu.SemaphoreType.DMA((down.shape[0] // width,)),
        ],
    )


def step_kernel(has, offsets, *refs):
    refs = list(refs)
    take = lambda: refs.pop(0)
    counts = {0: 1, 1: 3, 2: 4, 3: 2}
    inputs = {s: [take() for _ in range(counts[s])] for s in has}
    out_x, out_y = take(), take()
    if 0 in has:
        (send,) = inputs[0]
        at, size, _ = offsets[0]
        out_x[pl.ds(at, size)] = send[0]
        out_y[pl.ds(at, size)] = send[1]
    if 1 in has:
        keep, got_x, got_y = inputs[1]
        at, size, start = offsets[1]
        span = pl.ds(start, size)
        out_x[pl.ds(at, size)] = keep[1, 0].astype(bf16)
        out_x[pl.ds(at + size, size)] = (keep[1, 1] + got_y[span].astype(f32)).astype(bf16)
        out_y[pl.ds(at, size)] = (keep[2, 0] + got_x[span].astype(f32)).astype(bf16)
        out_y[pl.ds(at + size, size)] = keep[2, 1].astype(bf16)
    if 2 in has:
        keep, hidden, got_x, got_y = inputs[2]
        at, size, start = offsets[2]
        own = take()
        gate = keep[0, 0] + got_x[pl.ds(start, size)].astype(f32) + got_y[pl.ds(start, size)].astype(f32)
        upper = (
            keep[0, 1] + got_x[pl.ds(start + size, size)].astype(f32) + got_y[pl.ds(start + size, size)].astype(f32)
        )
        grad = hidden[...]
        sigma = jax.nn.sigmoid(gate)
        first = (grad * upper * sigma * (1.0 + gate * (1.0 - sigma))).astype(bf16)
        second = (grad * gate * sigma).astype(bf16)
        own[0] = first
        own[1] = second
        for out in (out_x, out_y):
            out[pl.ds(at, size)] = first
            out[pl.ds(at + size, size)] = second
    if 3 in has:
        got_x, got_y = inputs[3]
        at, size, start = offsets[3]
        out_x[pl.ds(at, size)] = got_y[pl.ds(start, size)]
        out_y[pl.ds(at, size)] = got_x[pl.ds(start + size, size)]


def gather_kernel(offset_one, offset_two, size, n, own, x_one, y_one, x_two, y_two, out):
    width = own.shape[2]
    for c in range(size // n):
        columns = pl.ds(c * width, width)
        rows = c * n
        for k in range(2):
            at = offset_one + k * size + rows
            out[k, pl.ds(0, n), columns] = own[k, pl.ds(rows, n)]
            out[k, pl.ds(n, n), columns] = x_one[pl.ds(at, n)]
            out[k, pl.ds(2 * n, n), columns] = y_one[pl.ds(at, n)]
        out[0, pl.ds(3 * n, n), columns] = x_two[pl.ds(offset_two + rows, n)]
        out[1, pl.ds(3 * n, n), columns] = y_two[pl.ds(offset_two + rows, n)]


class Exchange:
    def __init__(self, chain, units, lag, own_rows, width):
        self.chain, self.units, self.lag, self.width, self.own_rows = chain, units, lag, width, own_rows
        self.sends, self.keeps, self.hidden = {}, {}, {}
        self.got, self.place, self.own = {}, {}, {}

    def rows_in(self, u):
        return 2 * self.own_rows * len(self.units[u][0])

    def size_of(self, u):
        return (self.units[u][2] - self.units[u][1]) * self.rows_in(u)

    def stages(self, m):
        return {s: m - s * self.lag for s in range(4) if (m - s * self.lag) in self.units}

    def step(self, m):
        stages, lag = self.stages(m), self.lag
        pieces = (1, 2, 2, 1)
        offsets, at, operands = {}, 0, []
        for s, u in stages.items():
            size = self.size_of(u)
            offsets[s] = (at, size, self.place[u, s - 1] if s else 0)
            self.place[u, s] = at
            at += pieces[s] * size
            if s == 0:
                operands += [self.sends[u]]
            elif s == 1:
                operands += [self.keeps[u], *self.got[m - lag]]
            elif s == 2:
                operands += [self.keeps[u], self.hidden[u], *self.got[m - lag]]
            else:
                operands += [*self.got[m - lag]]
        shapes = [jax.ShapeDtypeStruct((at, self.width), bf16)] * 2
        if 2 in stages:
            shapes.append(jax.ShapeDtypeStruct((2, self.size_of(stages[2]), self.width), bf16))
        outs = self.chain.call(
            functools.partial(step_kernel, tuple(stages), offsets),
            [in_vmem] * len(operands),
            operands,
            [in_vmem] * len(shapes),
            shapes,
            "exchange_step",
            12,
            8 * at * self.width,
            8 * at * self.width,
        )
        self.got[m] = (swap(outs[0], 1), swap(outs[1], 2))
        if 2 in stages:
            self.own[stages[2]] = outs[2]

    def gather(self, u):
        n, columns = self.rows_in(u), (self.units[u][2] - self.units[u][1]) * self.width
        (out,) = self.chain.call(
            functools.partial(gather_kernel, self.place[u, 2], self.place[u, 3], self.size_of(u), n),
            [in_vmem] * 5,
            [self.own[u], *self.got[u + 2 * self.lag], *self.got[u + 3 * self.lag]],
            [in_vmem],
            [jax.ShapeDtypeStruct((2, 4 * n, columns), bf16)],
            "pre_grad",
            8,
            0,
            16 * n * columns,
        )
        return out


def shards(tokens, cotangent, gate_up, down_weight, first_code, first_scale, second_code, second_scale):
    groups = lax.axis_size("dp")
    bits = groups.bit_length() - 1
    chips = lax.axis_size("tensor") // 2
    me = lax.axis_index("dp")
    own, depth = tokens.shape
    rows, units = gate_up.shape[1:]
    width = 256 if units % 256 == 0 else 128
    chunks = units // width
    total_tokens = own * groups * lax.axis_size("tensor")
    orders = [list(range(bits)), list(reversed(range(bits)))]
    every = tuple(range(chips))
    rest = every[1:]
    staged = groups == 4 and chips == 4

    blocks = split_columns(tokens, groups, me)
    slots = [swap(block, s) if s else block for s, block in enumerate(blocks)]
    block = jnp.stack(slots)

    def near(value, axis, *others):
        return pack([(v, 0, v.shape[axis]) for v in (value, pair(value))], axis, *others)

    def send_on(value):
        return [onward(value, k) for k in rest]

    def far(found, axis, *others):
        n = found[0].shape[axis]
        other = pair(pack([(v, 0, n) for v in found], axis, *others))
        pieces = []
        for at, v in enumerate(found):
            pieces += [(v, 0, n), (other, at * n, at * n + n)]
        return pack(pieces, axis)

    packed = {((0,), 0): near(block, 1)}
    sent = send_on(block)
    packed[(0,), 1] = near(cotangent, 0, block)
    if not staged and rest:
        packed[rest, 0] = far(sent, 1)
        packed[rest, 1] = far(send_on(cotangent), 0)

    if staged:
        last = chunks - max(1, (chunks * 3) // 7)
        second = 7
        plan = {0: ((0,), 0, last)}
        plan[4] = (rest, 0, last)
        plan[second] = (every, last, chunks)
    else:
        plan = {c: (every, c, c + 1) for c in range(chunks)}

    def rows_of(ks):
        for kind in range(2):
            if (ks, kind) not in packed and (rest, kind) in packed:
                pieces = []
                for k in ks:
                    n = 2 * own
                    pieces.append((packed[(0,), kind], 0, n) if k == 0 else (packed[rest, kind], (k - 1) * n, k * n))
                packed[ks, kind] = pack(pieces, 1 - kind)
        t = packed[ks, 0]
        return (t, packed.get((ks, 1)), t.reshape(-1, rows))


    def forward(ks, c0, c1):
        t, c, _ = rows_of(ks)
        n = t.shape[1]
        lo, hi = c0 * width, c1 * width
        pre = []
        for k in range(2):
            w = gate_up[k, :, lo:hi]
            dot = lambda pick: jnp.dot(
                jnp.concatenate([t[s] for s in pick], axis=0), w, preferred_element_type=f32
            ).reshape(len(pick), n, hi - lo)
            active = list(range(groups))
            got = {s: [] for s in active}
            for b in orders[k]:
                mask = 1 << b
                send = [s for s in active if s & mask]
                active = [s for s in active if not s & mask]
                out = dot(send)
                for at, s in enumerate(send):
                    for extra in got[s]:
                        out = out.at[at].add(extra.astype(f32)) if len(send) > 1 else out + extra.astype(f32)[None]
                back = swap(out.astype(bf16), mask)
                for at, s in enumerate(send):
                    got[s ^ mask].append(back[at])
            value = dot([0])[0]
            for extra in got[0]:
                value = value + extra.astype(f32)
            pre.append(value)
        gate, upper = pre
        hidden = lax.dot_general(
            c, down_weight[lo:hi], (((1,), (1,)), ((), ())), preferred_element_type=f32
        )
        sigma = jax.nn.sigmoid(gate)
        grads = (
            (hidden * upper * sigma * (1.0 + gate * (1.0 - sigma))).astype(bf16),
            (hidden * gate * sigma).astype(bf16),
        )
        full = []
        for k in range(2):
            held = {0: grads[k]}
            for b in reversed(orders[k]):
                mask = 1 << b
                keys = sorted(held)
                back = swap(jnp.stack([held[s] for s in keys]), mask)
                for at, s in enumerate(keys):
                    held[s ^ mask] = back[at]
            full.append(jnp.concatenate([held[s] for s in range(groups)], axis=0))
        return jnp.stack(full)

    product = lambda g, c0, c1: jnp.einsum(
        "ktf,kdf->td", g, gate_up[:, :, c0 * width : c1 * width], preferred_element_type=f32
    )
    sums = {}

    def add_input_grad(u, g):
        ks, c0, c1 = plan[u]
        term = product(g, c0, c1)
        sums[ks] = term if ks not in sums else sums[ks] + term
        return sums[ks]

    def split(ks):
        value = sums[ks].reshape(groups, len(ks), 2, own, rows)
        return {k: value[:, at] for at, k in enumerate(ks)}

    def across(partial, ks):
        theirs = pair(jnp.stack([partial[k][:, 1] for k in ks]).astype(bf16))
        mine = [partial[k][:, 0] + theirs[at].astype(f32) for at, k in enumerate(ks)]
        return [back(v.astype(bf16), k).astype(f32) if k else v for k, v in zip(ks, mine)]

    def partials():
        partial = {}
        for ks in sums:
            for k, part in split(ks).items():
                partial[k] = partial[k] + part if k in partial else part
        return partial

    grads = {}
    if staged:
        chain = Chain()
        lag = 2
        exchange = Exchange(chain, plan, lag, own, width)
        steps = [m for m in range(max(plan) + 3 * lag + 1) if exchange.stages(m)]
        result, tops = [None], {}

        def input_grad_start():
            arrived = across(partials(), every)

            def wait():
                moved.append(sum(arrived).astype(bf16))
                chain.add(moved[0])

            return wait

        moved = []

        def start(u):
            exchange.sends[u], exchange.keeps[u] = partial_pre(
                chain, rows_of(plan[u][0])[2], gate_up, *plan[u][1:], width, 12 if u else 56
            )

        def hidden_first():
            return hidden_grad(chain, rows_of((0,))[1], down_weight, width, [(0, 2 * own, 0, last), (0, 2 * own, last, chunks)], 52)

        def hidden_rest(first, tail):
            n = 2 * own
            cuts = [(0, 3 * n, 0, last), (0, 3 * n, last, chunks)]
            found = hidden_grad(chain, rows_of(rest)[1], down_weight, width, cuts, 24)
            exchange.hidden[4] = found[0]
            both = [tail.reshape(chunks - last, n, width), found[1].reshape(chunks - last, 3 * n, width)]
            exchange.hidden[second] = pack([(v, 0, v.shape[1]) for v in both], 1).reshape(-1, width)

        def finish(u):
            grads[u] = exchange.gather(u)

        def inputs(u):
            chain.add(add_input_grad(u, grads[u]))

        def update(c0, c1, vmem):
            parts = []
            for u, (ks, a, b) in plan.items():
                if a <= c0 and c1 <= b:
                    parts.append((rows_of(ks)[2], grads[u], (c0 - a) * width))
            *result[0], tops[c0, 0], tops[c0, 1] = weight_step(
                chain, vmem, parts, gate_up, first_code, first_scale, second_code, second_scale, result[0], c0 * width, (c1 - c0) * width, total_tokens
            )

        start(0)
        for place, m in enumerate(steps):
            exchange.step(m)
            token = chain.tokens[0]
            if m == lag:
                packed[rest, 0] = far(sent, 1, token)
                exchange.hidden[0], hidden_tail = hidden_first()
            elif m == 2 * lag:
                cot_sent = send_on(hold_until(cotangent, token))
            elif m == 4 * lag - 1:
                packed[rest, 1] = far(cot_sent, 0, token)
                hidden_rest(exchange.hidden[0], hidden_tail)
            if place + 1 < len(steps) and steps[place + 1] in plan:
                start(steps[place + 1])
            if m == 4 * lag:
                finish(0)
                inputs(0)
            if m == second + 2 * lag:
                finish(4)
                inputs(4)
                update(0, last // 2, 20)
        finish(second)
        inputs(second)
        wait = input_grad_start()
        update(last // 2, last, 44)
        update(last, chunks - 1, 44)
        wait()
        update(chunks - 1, chunks, 44)
        outs = result[0]
        moved = moved[0]
    else:
        for u, unit in plan.items():
            grads[u] = forward(*unit)
            add_input_grad(u, grads[u])
        moved = sum(across(partials(), every), jnp.zeros((groups, own, rows), f32)).astype(bf16)

    final = jnp.stack([moved[0]] + [swap(moved[s], s) for s in range(1, groups)])
    final = jnp.stack([lax.dynamic_index_in_dim(final, me ^ a, 0, keepdims=False) for a in range(groups)], axis=1)
    input_grad = final.reshape(own, depth)

    if not staged:
        chain, outs, tops = Chain(), None, {}
        for c, (ks, c0, c1) in plan.items():
            *outs, tops[c0, 0], tops[c0, 1] = weight_step(
                chain,
                20,
                [(rows_of(ks)[2], grads[c], 0)],
                gate_up,
                first_code,
                first_scale,
                second_code,
                second_scale,
                outs,
                c0 * width,
                (c1 - c0) * width,
                total_tokens,
            )
    updated, code_one, code_two = outs
    scales = [jnp.concatenate([tops[c, i] for c, j in sorted(tops) if i == j], axis=0) for i in range(2)]
    scales = [jnp.transpose(scale, (1, 2, 0)) for scale in scales]
    return (input_grad, updated, code_one, scales[0], code_two, scales[1])


def solution(mesh):
    placed = (
        P(("dp", "tensor"), None),
        P(("dp", "tensor"), None),
        P(None, "dp", "tensor"),
        P("tensor", None),
        P(None, "dp", "tensor"),
        P(None, "dp", "tensor"),
        P(None, "dp", "tensor"),
        P(None, "dp", "tensor"),
    )
    return jax.shard_map(
        shards,
        mesh=mesh,
        in_specs=placed,
        out_specs=(
            P(("dp", "tensor"), None),
            P(None, "dp", "tensor"),
            P(None, "dp", "tensor"),
            P(None, "dp", "tensor"),
            P(None, "dp", "tensor"),
            P(None, "dp", "tensor"),
        ),
        check_vma=False,
    )
```
